512 devices in a mesh: grid: 32 (over x, z_hi, core), atom: 16 (over z_lo, y).
Axes of the slice: x: 4, y: 4, z: 16 (z_hi: 4, z_lo: 4; z = z_hi * 4 + z_lo), core: 2. Of those that a mesh axis runs over, the one named last changes fastest.
Arguments:
- basis_values: bfloat16 [1024, 128, 512], P(('grid', 'atom')), may hold values from -8 to 8
- block_lists: int32 [1024, 4], P('grid'), may hold values from 0 to 95, as said below
- orbitals: bfloat16 [12288, 4096], P('grid', 'atom'), may hold values from -0.00390625 to 0.00390625
- point_weights: float32 [131072], P(('grid', 'atom')), may hold values from 0.1 to 1
- point_atoms: int32 [131072], P(('grid', 'atom')), may hold values from 0 to 511, as said below
- embed_scale: float32 [256], replicated, may hold values from -4 to 4
- embed_shift: float32 [256], replicated, may hold values from -3 to 3
- message_weight: bfloat16 [2, 256, 256], replicated, may hold values from -0.375 to 0.375
- atom_weight: bfloat16 [2, 256, 256], replicated, may hold values from -0.375 to 0.375
- head_weight: float32 [256], replicated, may hold values from -0.375 to 0.375
Outputs:
- fock_orbitals: float32 [12288, 4096], P('grid', 'atom')
- potential: float32 [131072], P(('grid', 'atom'))
The draws below stay inside these ranges and needn't reach their ends.
Inputs may be any that keep to these rules, and one draw needn't show every extreme that they name: `block_lists`: each row names 4 different blocks; a batch b of group g = b // 32 names only blocks (g - 1) * 3 to (g + 2) * 3 - 1. `point_atoms`: the 256 points of one device name atom centres of one run of max(8, 1) consecutive centres, counted round.
All inputs are finite; a program needn't handle non-finite values.
Results may differ from the reference program's by a relative error of at most 0.04.
Values may be sent and summed in bfloat16 or wider, within the bound.
No kernel may reach another device: no remote copies, remote signals or barrier semaphores. Data moves between devices by JAX's collectives and lax.ppermute only.
A program may use at most 128 MiB of HBM per device.

```python
import math
import jax
import jax.numpy as jnp
from jax import lax

BLK = 128
NBLK = 96
NLIST = 4
BPTS = 128
NOCC = 4096
FEAT = 256
LAYERS = 2
PT_DEV = 256
ATOM_DEV = 32
NB = 12288
NATOM = 512
POINTS = 131072
NBATCH = 1024
N_GRID = 32


def draw_basis_values(key, part):
    owners = POINTS // PT_DEV
    per_owner = PT_DEV // BPTS
    key_scale = jax.random.fold_in(key, 21)
    key_entry = jax.random.fold_in(key, 22)
    exponent = jax.random.uniform(key_scale, (owners,), jnp.float32, -2.0, 1.5)
    owner_scale = jnp.repeat(jnp.exp(exponent), per_owner, total_repeat_length=NBATCH)
    entries = jax.random.normal(key_entry, (NBATCH, BPTS, NLIST * BLK), jnp.float32)
    batch_scale = jnp.ones((NBATCH,), jnp.float32)
    values = entries * (owner_scale * batch_scale)[:, None, None]
    return jnp.clip(values, -8.0, 8.0).astype(jnp.bfloat16)


def draw_block_lists(key, part):
    per_group = NBATCH // N_GRID
    owned = NBLK // N_GRID
    span = 3 * owned
    group = jnp.arange(NBATCH, dtype=jnp.int32) // per_group
    base = (group - 1) * owned
    offsets = jnp.arange(span, dtype=jnp.int32)
    positions = base[:, None] + offsets[None, :]
    outside = jnp.logical_or(positions < 0, positions >= NBLK).astype(jnp.int32)
    scores = jax.random.randint(key, (NBATCH, span), 0, 1048576, dtype=jnp.int32) * span + offsets[None, :]
    scores = scores + outside * 67108864
    order = jnp.argsort(scores, axis=1, stable=True).astype(jnp.int32)
    return base[:, None] + order[:, :NLIST]


def draw_point_atoms(key, part):
    key_start = jax.random.fold_in(key, 11)
    key_first = jax.random.fold_in(key, 12)
    key_second = jax.random.fold_in(key, 13)
    owners = POINTS // PT_DEV
    window = max(ATOM_DEV // 4, 1)
    starts = jax.random.randint(key_start, (owners,), 0, NATOM, dtype=jnp.int32)
    first = jax.random.randint(key_first, (owners, PT_DEV), 0, window, dtype=jnp.int32)
    second = jax.random.randint(key_second, (owners, PT_DEV), 0, window, dtype=jnp.int32)
    picked = jnp.minimum(first, second)
    return ((starts[:, None] + picked) % NATOM).reshape(-1).astype(jnp.int32)


def steps_of(own_key, shape, split, low, high):
    factor_of, own = 1.0, jax.random.fold_in(own_key, 6)
    for position, shards_of in split:
        heights = jnp.exp(jax.random.uniform(jax.random.fold_in(own, position), (shards_of,), jnp.float32, low / len(split), high / len(split)))
        factor_of = factor_of * jnp.repeat(heights, shape[position] // shards_of).reshape([-1 if axis == position else 1 for axis in range(len(shape))])
    return factor_of


def gaussian(own_key, dims, scale, most, shards=(), kind=jnp.bfloat16):
    result = jax.random.normal(own_key, dims, jnp.float32) * scale
    if len(shards) > 0:
        result = steps_of(own_key, dims, shards, -0.22, 0.18) * result
    return jnp.clip(result, min=-most, max=most).astype(kind)


def setup_inputs(seed: int = 0) -> dict:
    keys = jax.random.split(jax.random.key(seed), 11)
    return {
        "basis_values": draw_basis_values(jax.random.fold_in(keys[10], 71), 0),
        "block_lists": draw_block_lists(jax.random.fold_in(keys[10], 71), 0),
        "orbitals": gaussian(keys[2], (NB, NOCC), (NLIST * BLK * NOCC) ** -0.5, 0.00390625, ((0, 32), (1, 16))),
        "point_weights": jnp.clip(jnp.exp(math.log(1.0) - 2.3025851 * jax.random.uniform(keys[3], (POINTS,), jnp.float32) ** steps_of(keys[3], (POINTS,), ((0, 512),), -0.2, 0.2)), 0.1, 1.0),
        "point_atoms": draw_point_atoms(jax.random.fold_in(keys[10], 71), 0),
        "embed_scale": gaussian(keys[5], (FEAT,), 1.0, 4.0, (), jnp.float32),
        "embed_shift": gaussian(keys[6], (FEAT,), 0.7, 3.0, (), jnp.float32),
        "message_weight": gaussian(keys[7], (LAYERS, FEAT, FEAT), FEAT ** -0.5, 0.375),
        "atom_weight": gaussian(keys[8], (LAYERS, FEAT, FEAT), FEAT ** -0.5, 0.375),
        "head_weight": gaussian(keys[9], (FEAT,), FEAT ** -0.5, 0.375, (), jnp.float32),
    }


def orbital_values(values, lists, orbitals):
    blocks = orbitals.reshape(NBLK, BLK, NOCC)
    chosen = blocks[lists].reshape(lists.shape[0], NLIST * BLK, NOCC)
    psi = jnp.einsum("bpk,bko->bpo", values.astype(jnp.float32), chosen.astype(jnp.float32))
    return psi.astype(jnp.bfloat16)


def reference(basis_values, block_lists, orbitals, point_weights, point_atoms, embed_scale, embed_shift, message_weight, atom_weight, head_weight):
    grouped_values = basis_values.reshape(N_GRID, -1, BPTS, NLIST * BLK)
    grouped_lists = block_lists.reshape(N_GRID, -1, NLIST)

    def group_density(items):
        psi = orbital_values(items[0], items[1], orbitals)
        return 2.0 * jnp.sum(jnp.square(psi.astype(jnp.float32)), axis=2)

    density = lax.map(group_density, (grouped_values, grouped_lists)).reshape(-1)
    radius = jnp.cbrt(density)
    hidden = jax.nn.silu(radius[:, None] * embed_scale[None, :] + embed_shift[None, :])
    mass = jax.ops.segment_sum(point_weights, point_atoms, num_segments=NATOM)
    for layer in range(LAYERS):
        message = jax.nn.silu(jnp.dot(hidden.astype(jnp.bfloat16), message_weight[layer], preferred_element_type=jnp.float32))
        weighted = (point_weights[:, None] * message).astype(jnp.bfloat16)
        rows = jax.ops.segment_sum(weighted.astype(jnp.float32), point_atoms, num_segments=NATOM)
        mean = rows / (1.0 + mass[:, None])
        update = jax.nn.silu(jnp.dot(mean.astype(jnp.bfloat16), atom_weight[layer], preferred_element_type=jnp.float32)).astype(jnp.bfloat16)
        hidden = hidden + message * update[point_atoms].astype(jnp.float32)
    score = jnp.dot(hidden, head_weight, precision=lax.Precision.HIGHEST)
    potential = radius * (1.0 + jnp.tanh(score))
    scaled = (point_weights * potential).reshape(N_GRID, -1, BPTS)

    def group_fock(total, items):
        values, lists, scale = items
        psi = orbital_values(values, lists, orbitals)
        weighted_psi = (scale[:, :, None] * psi.astype(jnp.float32)).astype(jnp.bfloat16)
        terms = jnp.einsum("bpk,bpo->bko", values.astype(jnp.float32), weighted_psi.astype(jnp.float32))
        terms = terms.reshape(-1, BLK, NOCC)
        partial_value = jnp.zeros((NBLK, BLK, NOCC), jnp.float32).at[lists.reshape(-1)].add(terms)
        rounded = lax.optimization_barrier(partial_value.astype(jnp.bfloat16)).astype(jnp.float32)
        return total + rounded, None

    start = jnp.zeros((NBLK, BLK, NOCC), jnp.float32)
    total, unused = lax.scan(group_fock, start, (grouped_values, grouped_lists, scaled))
    return total.reshape(NB, NOCC), potential
```

```python
import jax
import jax.numpy as jnp
from jax import lax
from jax.experimental import pallas as pl
from jax.experimental.pallas import tpu as pltpu
from jax.sharding import Mesh
from jax.sharding import PartitionSpec as P

AXES = ("x", "zh", "c", "zl", "y")
GRID = ("x", "zh", "c")
PLANE = ("x", "c", "y")
COLUMN = ("zh", "zl")
SIDE = 4
BLK = 128
WINDOW = 8
NATOM = 512
ROWS = 16
F32 = jnp.float32
BF16 = jnp.bfloat16

VMEM = 48 * 1024 * 1024


def call(kernel, out_shape, n_in, smem=(), scratch=(), **kw):
    specs = [
        pl.BlockSpec(memory_space=pltpu.SMEM if i in smem else pltpu.VMEM) for i in range(n_in)
    ]
    outs = jax.tree.map(lambda _: pl.BlockSpec(memory_space=pltpu.VMEM), out_shape)
    return pl.pallas_call(
        kernel,
        out_shape=out_shape,
        in_specs=specs,
        out_specs=outs,
        scratch_shapes=list(scratch),
        compiler_params=pltpu.CompilerParams(vmem_limit_bytes=VMEM),
        **kw,
    )


def shape(dims, dtype):
    return jax.ShapeDtypeStruct(dims, dtype)


def spread_kernel(place_ref, row_ref, *refs):
    parts, (dense_ref, flipped_ref) = refs[:SIDE], refs[SIDE:]
    dense_ref[...] = jnp.zeros_like(dense_ref)
    flipped_ref[...] = jnp.zeros_like(flipped_ref)
    for k, part in enumerate(parts):
        for r in range(part.shape[0]):
            n = k * part.shape[0] + r
            row = pl.multiple_of(row_ref[n] * BLK, BLK)
            for j in range(part.shape[2] // BLK):
                col = pl.multiple_of(place_ref[n, j] * BLK, BLK)
                tile = part[r, :, j * BLK : (j + 1) * BLK]
                dense_ref[pl.ds(row, BLK), pl.ds(col, BLK)] = tile
                flipped_ref[pl.ds(col, BLK), pl.ds(row, BLK)] = tile.T


def psi_kernel(dense_ref, *refs):
    own, outer = refs[:SIDE], refs[SIDE : 2 * SIDE]
    partner, psi_ref, dens_ref, acc_ref = refs[2 * SIDE :]
    width = own[0].shape[1]
    for k in range(SIDE):
        chosen = jnp.concatenate([own[k][...], outer[k][...], partner[k]], axis=0)
        psi = jnp.dot(dense_ref[...], chosen, preferred_element_type=F32).astype(BF16)
        psi_ref[:, k * width : (k + 1) * width] = psi
        wide = psi.astype(F32)
        square = wide * wide
        part = square[:, :BLK] + square[:, BLK:]
        if k == 0:
            acc_ref[...] = part
        else:
            acc_ref[...] += part
    for n in range(acc_ref.shape[0] // BLK):
        tile = acc_ref[n * BLK : (n + 1) * BLK, :].T
        dens_ref[n // 2, n % 2 : n % 2 + 1, :] = 2.0 * jnp.sum(tile, axis=0, keepdims=True)


def silu(x):
    return x * jax.nn.sigmoid(x)


def column(tall, n):
    return jnp.concatenate([tall[:, n : n + 1], tall[:, n + 1 : n + 2]], axis=0)


def message_of(hidden, weight, weights_col, selector, meta):
    message = silu(jnp.dot(hidden.astype(BF16), weight, preferred_element_type=F32))
    weighted = (weights_col * message).astype(BF16)
    rows = jnp.dot(selector, weighted, preferred_element_type=F32)
    return message, (rows + meta).astype(BF16)


def first_kernel(
    radius_ref, pw_ref, scale_ref, shift_ref, weight_ref, sel_ref, meta_ref,
    hidden_ref, message_ref, cols_ref, out_ref, scratch,
):
    scratch[...] = jnp.zeros_like(scratch)
    scratch[0:2, :] = radius_ref[...]
    scratch[2:4, :] = pw_ref[...]
    tall = scratch[...].T
    cols_ref[...] = tall
    radius, weights = column(tall, 0), column(tall, 2)
    hidden = silu(radius * scale_ref[...] + shift_ref[...])
    hidden_ref[...] = hidden
    message, payload = message_of(hidden, weight_ref[0], weights, sel_ref[...], meta_ref[...])
    message_ref[...] = message
    out_ref[...] = jnp.broadcast_to(payload[None], out_ref.shape)


def route_first_kernel(x_ref, target_ref, out_ref, match_ref):
    n = x_ref.shape[0] * ROWS
    x = x_ref[...].reshape(n, x_ref.shape[2])
    meta = x[:, :BLK].astype(F32)
    meta = jnp.concatenate([meta[WINDOW:], meta[:WINDOW]], axis=0)
    atom = meta[:, 1:2] * 16.0 + meta[:, 2:3]
    row = lax.broadcasted_iota(jnp.int32, (n, BLK), 0)
    valid = lax.rem(row, ROWS) < WINDOW
    match = jnp.where(jnp.logical_and(atom == target_ref[...], valid), 1.0, 0.0).astype(BF16)
    match_ref[...] = match
    down = (((0,), (0,)), ((), ()))
    sums = lax.dot_general(match, x, down, preferred_element_type=F32)
    mass = lax.dot_general(match, meta.astype(BF16), down, preferred_element_type=F32)
    count = out_ref.shape[0]
    mass = jnp.concatenate([mass, jnp.zeros_like(mass)], axis=1)
    both = jnp.concatenate(
        [sums.reshape(count, WINDOW, -1), mass.reshape(count, WINDOW, -1)], axis=1
    )
    out_ref[...] = both.astype(BF16)


def route_kernel(x_ref, match_ref, out_ref):
    x = x_ref[...].reshape(x_ref.shape[0] * ROWS, x_ref.shape[2])
    down = (((0,), (0,)), ((), ()))
    sums = lax.dot_general(match_ref[...], x, down, preferred_element_type=F32)
    sums = sums.reshape(out_ref.shape[0], WINDOW, -1)
    out_ref[...] = jnp.concatenate([sums, jnp.zeros_like(sums)], axis=1).astype(BF16)


def updated(rows, mass, weight, hidden, message, spread):
    mean = rows / (1.0 + mass)
    mean = jnp.concatenate([mean, jnp.zeros_like(mean)], axis=0).astype(BF16)
    update = silu(jnp.dot(mean, weight, preferred_element_type=F32)).astype(BF16)
    filler = jnp.zeros((BLK - ROWS, update.shape[1]), BF16)
    update = jnp.concatenate([update, filler], axis=0)
    picked = jnp.dot(spread, update, preferred_element_type=F32)
    return hidden + message * picked


def second_kernel(
    z_ref, atom_weight_ref, weight_ref, hidden_ref, message_ref, cols_ref, spread_ref, sel_ref,
    hidden_out, message_out, mass_ref, out_ref,
):
    total = jnp.sum(z_ref[...].astype(F32), axis=0)
    mass = jnp.broadcast_to(total[WINDOW:, 0:1], mass_ref.shape)
    mass_ref[...] = mass
    hidden = updated(
        total[:WINDOW], mass[:, 0:1], atom_weight_ref[0], hidden_ref[...], message_ref[...],
        spread_ref[...],
    )
    hidden_out[...] = hidden
    weights = column(cols_ref[...], 2)
    message, payload = message_of(hidden, weight_ref[1], weights, sel_ref[...], 0.0)
    message_out[...] = message
    out_ref[...] = jnp.broadcast_to(payload[None], out_ref.shape)


def last_kernel(
    z_ref, mass_ref, atom_weight_ref, hidden_ref, message_ref, cols_ref, spread_ref, head_ref,
    potential_ref, scaled_ref,
):
    total = jnp.sum(z_ref[...].astype(F32), axis=0)
    hidden = updated(
        total[:WINDOW], mass_ref[:, 0:1], atom_weight_ref[1], hidden_ref[...], message_ref[...],
        spread_ref[...],
    )
    score = jnp.sum(hidden * head_ref[...], axis=1, keepdims=True)
    radius, weights = column(cols_ref[...], 0), column(cols_ref[...], 2)
    potential = radius * (1.0 + jnp.tanh(score))
    scaled = weights * potential
    lane = lax.broadcasted_iota(jnp.int32, (BLK, BLK), 1)
    flat = jnp.where(lane == 0, potential[:BLK], 0.0)
    flat = jnp.where(lane == 1, potential[BLK:], flat)
    flat = jnp.where(lane == 2, scaled[:BLK], flat)
    flat = jnp.where(lane == 3, scaled[BLK:], flat)
    flat = flat.T
    potential_ref[...] = flat[0:2]
    for k in range(scaled_ref.shape[0]):
        scaled_ref[k] = flat[2:4]


def fock_kernel(flipped_ref, psi_ref, scaled_ref, *refs):
    own, outer = refs[:SIDE], refs[SIDE : 2 * SIDE]
    partner, weighted, scratch = refs[2 * SIDE :]
    for k in range(SIDE):
        scratch[2 * k : 2 * k + 2, :] = scaled_ref[k]
    tall = scratch[...].T
    for n in range(2 * SIDE):
        rows = slice(n * BLK, (n + 1) * BLK)
        weighted[rows, :] = (tall[:, n : n + 1] * psi_ref[rows, :].astype(F32)).astype(BF16)
    deep, width = own[0].shape
    for k in range(SIDE):
        terms = jnp.dot(
            flipped_ref[...], weighted[:, k * width : (k + 1) * width], preferred_element_type=F32
        ).astype(BF16)
        own[k][...] = terms[:deep]
        outer[k][...] = terms[deep : 2 * deep]
        partner[k] = terms[2 * deep :]


def turn(axis, step):
    return [(i, (i + step) % SIDE) for i in range(SIDE)]


def across(value):
    groups = lax.axis_size(GRID)
    pairs = [(g, g + 1 if g % 2 else g - 1) for g in range(1, groups - 1)]
    return lax.ppermute(value, GRID, pairs)


def swap(value):
    return lax.ppermute(value, "c", [(0, 1), (1, 0)])


def exchange(parts, axes):
    return lax.all_to_all(parts, axes, split_axis=0, concat_axis=0, tiled=True)


def local(
    basis_values,
    block_lists,
    orbitals,
    point_weights,
    point_atoms,
    embed_scale,
    embed_shift,
    message_weight,
    atom_weight,
    head_weight,
):
    feat = embed_scale.shape[0]
    points = point_weights.shape[0]
    batches, batch_points, _ = basis_values.shape
    deep, width = orbitals.shape
    owned = deep // BLK
    core, zl, y = lax.axis_index("c"), lax.axis_index("zl"), lax.axis_index("y")
    group = lax.axis_index(GRID)
    plane, column_size = lax.axis_size(PLANE), lax.axis_size(COLUMN)

    across_rows = across(orbitals)
    own = [orbitals] + [lax.ppermute(orbitals, "y", turn("y", k)) for k in range(1, SIDE)]
    parts = [basis_values] + [
        lax.ppermute(basis_values, "zl", turn("zl", k)) for k in range(1, SIDE)
    ]
    outer = [across_rows] + [lax.ppermute(across_rows, "y", turn("y", k)) for k in range(1, SIDE)]
    partner = swap(jnp.stack(own))

    first = point_atoms[0]
    half = NATOM // 2
    lowest = jnp.min((point_atoms - first + half + NATOM) % NATOM - half)
    start = (first + lowest + NATOM) % NATOM
    slot = (point_atoms - start + NATOM) % NATOM
    selector = (jnp.arange(ROWS, dtype=jnp.int32)[:, None] == slot[None, :]).astype(BF16)
    spread = (slot[:, None] == jnp.arange(BLK, dtype=jnp.int32)[None, :]).astype(BF16)
    window = (start + jnp.arange(WINDOW, dtype=jnp.int32)) % NATOM
    mass = jnp.sum(
        jnp.where(jnp.arange(WINDOW)[:, None] == slot[None, :], point_weights[None, :], 0.0), axis=1
    )
    facts = jnp.stack([mass, (window // 16).astype(F32), (window % 16).astype(F32)], axis=1)
    meta = jnp.zeros((ROWS, feat), F32).at[WINDOW:, :3].set(facts)
    targets = exchange(jnp.broadcast_to(window.astype(F32), (column_size, WINDOW)), COLUMN)
    targets = targets.reshape(1, column_size * WINDOW)

    shift_k = jnp.arange(SIDE, dtype=jnp.int32)
    from_zl = (zl - shift_k + SIDE) % SIDE
    batch = (from_zl * SIDE + y)[:, None] * batches + jnp.arange(batches, dtype=jnp.int32)[None, :]
    batch = batch.reshape(-1)
    lists = block_lists[batch] - (group - 1) * owned
    third = lists // owned
    low = jnp.where(core == 0, 1, 2)
    place = jnp.where(third == 1, 0, jnp.where(third == 0, low, 3 - low)) * owned + lists % owned
    row = (from_zl[:, None] * batches + jnp.arange(batches, dtype=jnp.int32)[None, :]).reshape(-1)

    total_points = SIDE * points
    dense, flipped = call(
        spread_kernel,
        (shape((total_points, 3 * deep), BF16), shape((3 * deep, total_points), BF16)),
        2 + SIDE,
        smem=(0, 1),
    )(place.astype(jnp.int32), row, *parts)

    psi, squares = call(
        psi_kernel,
        (
            shape((total_points, SIDE * width), BF16),
            shape((SIDE, batches, batch_points), F32),
        ),
        2 + 2 * SIDE,
        scratch=[pltpu.VMEM((total_points, BLK), F32)],
    )(dense, *own, *outer, partner)
    density = jnp.sum(exchange(squares, ("zl",)), axis=0)
    radius = jnp.cbrt(density)

    weights = point_weights.reshape(batches, batch_points)
    square_f32 = shape((points, feat), F32)
    to_plane = shape((plane, ROWS, feat), BF16)
    to_column = shape((column_size, ROWS, feat), BF16)
    tall = shape((batch_points, 8), F32)
    hidden, message, cols, sent = call(
        first_kernel,
        (square_f32, square_f32, tall, to_plane),
        7,
        scratch=[pltpu.VMEM((8, batch_points), F32)],
    )(radius, weights, embed_scale[None], embed_shift[None], message_weight, selector, meta)
    sums, match = call(
        route_first_kernel, (to_column, shape((plane * ROWS, BLK), BF16)), 2
    )(exchange(sent, PLANE), targets)
    hidden, message, mass_rows, sent = call(
        second_kernel, (square_f32, square_f32, shape((WINDOW, BLK), F32), to_plane), 8
    )(
        exchange(sums, COLUMN), atom_weight, message_weight, hidden, message, cols, spread, selector
    )
    sums = call(route_kernel, to_column, 2)(exchange(sent, PLANE), match)
    potential, scaled = call(
        last_kernel,
        (shape((batches, batch_points), F32), shape((SIDE, batches, batch_points), F32)),
        8,
    )(
        exchange(sums, COLUMN), mass_rows, atom_weight, hidden, message, cols, spread,
        head_weight[None],
    )
    scaled = exchange(scaled, ("zl",))

    piece = shape((deep, width), BF16)
    *terms, for_partner = call(
        fock_kernel,
        tuple([piece] * (2 * SIDE) + [shape((SIDE, deep, width), BF16)]),
        3,
        scratch=[
            pltpu.VMEM((total_points, SIDE * width), BF16),
            pltpu.VMEM((8, batch_points), F32),
        ],
    )(flipped, psi, scaled)
    own_terms, outer_terms = terms[:SIDE], terms[SIDE:]

    outer_back = [outer_terms[0]] + [
        lax.ppermute(outer_terms[k], "y", turn("y", -k)) for k in range(1, SIDE)
    ]
    swapped = swap(for_partner)
    outer_sum = sum(t.astype(F32) for t in outer_back).astype(BF16)
    arrived = across(outer_sum)
    both = [own_terms[k].astype(F32) + swapped[k].astype(F32) for k in range(SIDE)]
    back = [
        lax.ppermute(both[k].astype(BF16), "y", turn("y", -k)).astype(F32) for k in range(1, SIDE)
    ]
    fock = both[0] + back[0] + back[1] + back[2] + arrived.astype(F32)
    return fock, potential.reshape(-1)


def solution(mesh):
    finer = Mesh(mesh.devices.reshape(4, 4, 2, 4, 4), AXES)
    atom = ("zl", "y")
    placed = (
        P(AXES, None, None),
        P(GRID, None),
        P(GRID, atom),
        P(AXES),
        P(AXES),
        P(),
        P(),
        P(),
        P(),
        P(),
    )
    return jax.shard_map(
        local,
        mesh=finer,
        in_specs=placed,
        out_specs=(P(GRID, atom), P(AXES)),
        check_vma=False,
    )
```

```python
import jax
import jax.numpy as jnp
from jax import lax
from jax.experimental import pallas as pl
from jax.experimental.pallas import tpu as pltpu
from jax.sharding import Mesh
from jax.sharding import PartitionSpec as P

AXES = ("x", "zh", "c", "zl", "y")
GRID = ("x", "zh", "c")
PLANE = ("x", "c", "y")
COLUMN = ("zh", "zl")
SIDE = 4
BLK = 128
WINDOW = 8
NATOM = 512
ROWS = 16
F32 = jnp.float32
BF16 = jnp.bfloat16

VMEM = 16 * 1024 * 1024


def call(kernel, out_shape, n_in, smem=(), scratch=(), **kw):
    specs = [
        pl.BlockSpec(memory_space=pltpu.SMEM if i in smem else pltpu.VMEM) for i in range(n_in)
    ]
    outs = jax.tree.map(lambda _: pl.BlockSpec(memory_space=pltpu.VMEM), out_shape)
    return pl.pallas_call(
        kernel,
        out_shape=out_shape,
        in_specs=specs,
        out_specs=outs,
        scratch_shapes=list(scratch),
        compiler_params=pltpu.CompilerParams(vmem_limit_bytes=VMEM),
        **kw,
    )


def shape(dims, dtype):
    return jax.ShapeDtypeStruct(dims, dtype)


def prepare_kernel(atoms_ref, weights_ref, sel_ref, spread_ref, meta_ref, window_ref, scratch):
    atoms = atoms_ref[...].astype(F32)
    half = NATOM // 2
    first = atoms[0:1, 0:1]
    apart = atoms - first
    apart = jnp.where(apart < -half, apart + NATOM, jnp.where(apart >= half, apart - NATOM, apart))
    start = first + jnp.min(jnp.min(apart, axis=1, keepdims=True), axis=0, keepdims=True)
    start = jnp.where(start < 0, start + NATOM, jnp.where(start >= NATOM, start - NATOM, start))
    slot = atoms - start
    slot = jnp.where(slot < 0, slot + NATOM, slot)
    points = 2 * BLK
    wide = jnp.concatenate([slot[0:1], slot[1:2]], axis=1)
    weights = jnp.concatenate([weights_ref[0:1], weights_ref[1:2]], axis=1)
    rows = lax.broadcasted_iota(jnp.int32, (ROWS, points), 0).astype(F32)
    chosen = rows == wide
    sel_ref[...] = jnp.where(chosen, 1.0, 0.0).astype(BF16)
    scratch[...] = jnp.zeros_like(scratch)
    scratch[0:2, :] = slot
    tall = scratch[...].T
    lanes = lax.broadcasted_iota(jnp.int32, (points, BLK), 1).astype(F32)
    spread_ref[...] = jnp.where(lanes == column(tall, 0), 1.0, 0.0).astype(BF16)
    mass = jnp.sum(jnp.where(chosen, weights, 0.0), axis=1, keepdims=True)[:WINDOW]
    atom = start + lax.broadcasted_iota(jnp.int32, (WINDOW, 1), 0).astype(F32)
    atom = jnp.where(atom >= NATOM, atom - NATOM, atom)
    high = jnp.floor(atom * (1.0 / 16.0))
    low = atom - 16.0 * high
    lane = lax.broadcasted_iota(jnp.int32, (WINDOW, points), 1)
    facts = jnp.where(lane == 0, mass, jnp.where(lane == 1, high, jnp.where(lane == 2, low, 0.0)))
    meta_ref[...] = jnp.concatenate([jnp.zeros_like(facts), facts], axis=0)
    row = lax.broadcasted_iota(jnp.int32, window_ref.shape, 0)
    window_ref[...] = jnp.where(
        row == 0, high[0:1], jnp.where(row == 1, low[0:1], 0.0)
    ).astype(BF16)


def spread_kernel(place_ref, list_ref, *refs):
    parts, (dense_ref, flipped_ref) = refs[:SIDE], refs[SIDE:]
    zl, y, group, core = (place_ref[i] for i in range(4))
    dense_ref[...] = jnp.zeros_like(dense_ref)
    flipped_ref[...] = jnp.zeros_like(flipped_ref)
    per, _, wide = parts[0].shape
    owned = dense_ref.shape[1] // BLK // 3
    for k, part in enumerate(parts):
        origin = lax.rem(zl - k + SIDE, SIDE)
        for r in range(per):
            batch = (origin * SIDE + y) * per + r
            row = pl.multiple_of((origin * per + r) * BLK, BLK)
            for j in range(wide // BLK):
                block = list_ref[batch, j] - (group - 1) * owned
                below, above = block < owned, block >= 2 * owned
                outside = jnp.logical_or(below, above)
                outer = below == (core == 0)
                within = jnp.where(below, block, jnp.where(above, block - 2 * owned, block - owned))
                third = jnp.where(outside, jnp.where(outer, 1, 2), 0)
                col = pl.multiple_of((third * owned + within) * BLK, BLK)
                tile = part[r, :, j * BLK : (j + 1) * BLK]
                dense_ref[pl.ds(row, BLK), pl.ds(col, BLK)] = tile
                flipped_ref[pl.ds(col, BLK), pl.ds(row, BLK)] = tile.T


def psi_kernel(place_ref, dense_ref, rows_ref, psi_ref, dens_ref, acc_ref):
    _, _, _, core, x = (place_ref[i] for i in range(5))
    side, tall, width = rows_ref.shape
    deep = dense_ref.shape[1] // 3
    lane = lax.broadcasted_iota(jnp.int32, (1, BLK), 1)
    device = lane // WINDOW
    atoms = (lane % WINDOW).astype(F32)
    for k in range(side):
        chosen = jnp.concatenate(
            [rows_ref[k, :deep], rows_ref[k, deep + ROWS : tall - ROWS]], axis=0
        )
        psi = jnp.dot(dense_ref[...], chosen, preferred_element_type=F32).astype(BF16)
        psi_ref[:, k * width : (k + 1) * width] = psi
        wide = psi.astype(F32)
        square = wide * wide
        part = square[:, :BLK] + square[:, BLK:]
        if k == 0:
            acc_ref[...] = part
        else:
            acc_ref[...] += part
        for at, owner in ((deep, core), (tall - ROWS, 1 - core)):
            window = rows_ref[k, at : at + ROWS, :BLK].astype(F32)
            window = window[0:1] * 16.0 + window[1:2]
            atoms += jnp.where(device == owner * side + k, window, 0.0)
    atoms = jnp.where(atoms >= NATOM, atoms - NATOM, atoms)
    atoms = jnp.where(device < 2 * side, atoms, 0.0)
    dens_ref[...] = jnp.zeros_like(dens_ref)
    for n in range(dens_ref.shape[0]):
        dens_ref[n, 2:3, :] = atoms
    for n in range(acc_ref.shape[0] // BLK):
        tile = acc_ref[n * BLK : (n + 1) * BLK, :].T
        row = 2.0 * jnp.sum(tile, axis=0, keepdims=True)
        dens_ref[x * side + n // 2, n % 2 : n % 2 + 1, :] = row


def silu(x):
    return x * jax.nn.sigmoid(x)


def column(tall, n):
    return jnp.concatenate([tall[:, n : n + 1], tall[:, n + 1 : n + 2]], axis=0)


def message_of(hidden, weight, weights_col, selector, meta):
    message = silu(jnp.dot(hidden.astype(BF16), weight, preferred_element_type=F32))
    weighted = (weights_col * message).astype(BF16)
    rows = jnp.dot(selector, weighted, preferred_element_type=F32)
    return message, (rows + meta).astype(BF16)


def first_kernel(
    radius_ref, pw_ref, scale_ref, shift_ref, weight_ref, sel_ref, meta_ref,
    hidden_ref, message_ref, cols_ref, out_ref, scratch,
):
    scratch[...] = jnp.zeros_like(scratch)
    scratch[0:2, :] = radius_ref[...]
    scratch[2:4, :] = pw_ref[...]
    tall = scratch[...].T
    cols_ref[...] = tall
    radius, weights = column(tall, 0), column(tall, 2)
    hidden = silu(radius * scale_ref[...] + shift_ref[...])
    hidden_ref[...] = hidden
    message, payload = message_of(hidden, weight_ref[0], weights, sel_ref[...], meta_ref[...])
    message_ref[...] = message
    out_ref[...] = jnp.broadcast_to(payload[None], out_ref.shape)


def route_first_kernel(place_ref, x_ref, target_ref, out_ref, match_ref):
    n = x_ref.shape[0] * ROWS
    zl = place_ref[0]
    half = [target_ref[k * SIDE + zl, 2:3, :] for k in range(SIDE)]
    targets = jnp.concatenate(
        [half[0] + pltpu.roll(half[1], BLK // 2, 1), half[2] + pltpu.roll(half[3], BLK // 2, 1)],
        axis=1,
    )
    x = x_ref[...].reshape(n, x_ref.shape[2])
    meta = x[:, :BLK].astype(F32)
    meta = jnp.concatenate([meta[WINDOW:], meta[:WINDOW]], axis=0)
    atom = meta[:, 1:2] * 16.0 + meta[:, 2:3]
    row = lax.broadcasted_iota(jnp.int32, (n, targets.shape[1]), 0)
    valid = lax.rem(row, ROWS) < WINDOW
    match = jnp.where(jnp.logical_and(atom == targets, valid), 1.0, 0.0).astype(BF16)
    match_ref[...] = match
    down = (((0,), (0,)), ((), ()))
    sums = lax.dot_general(match, x, down, preferred_element_type=F32)
    mass = lax.dot_general(match, meta.astype(BF16), down, preferred_element_type=F32)
    count = out_ref.shape[0]
    mass = jnp.concatenate([mass, jnp.zeros_like(mass)], axis=1)
    both = jnp.concatenate(
        [sums.reshape(count, WINDOW, -1), mass.reshape(count, WINDOW, -1)], axis=1
    )
    out_ref[...] = both.astype(BF16)


def route_kernel(x_ref, match_ref, out_ref):
    x = x_ref[...].reshape(x_ref.shape[0] * ROWS, x_ref.shape[2])
    down = (((0,), (0,)), ((), ()))
    sums = lax.dot_general(match_ref[...], x, down, preferred_element_type=F32)
    sums = sums.reshape(out_ref.shape[0], WINDOW, -1)
    out_ref[...] = jnp.concatenate([sums, jnp.zeros_like(sums)], axis=1).astype(BF16)


def updated(rows, mass, weight, hidden, message, spread):
    mean = rows / (1.0 + mass)
    mean = jnp.concatenate([mean, jnp.zeros_like(mean)], axis=0).astype(BF16)
    update = silu(jnp.dot(mean, weight, preferred_element_type=F32)).astype(BF16)
    filler = jnp.zeros((BLK - ROWS, update.shape[1]), BF16)
    update = jnp.concatenate([update, filler], axis=0)
    picked = jnp.dot(spread, update, preferred_element_type=F32)
    return hidden + message * picked


def second_kernel(
    z_ref, atom_weight_ref, weight_ref, hidden_ref, message_ref, cols_ref, spread_ref, sel_ref,
    hidden_out, message_out, mass_ref, out_ref,
):
    total = jnp.sum(z_ref[...].astype(F32), axis=0)
    mass = jnp.broadcast_to(total[WINDOW:, 0:1], mass_ref.shape)
    mass_ref[...] = mass
    hidden = updated(
        total[:WINDOW], mass[:, 0:1], atom_weight_ref[0], hidden_ref[...], message_ref[...],
        spread_ref[...],
    )
    hidden_out[...] = hidden
    weights = column(cols_ref[...], 2)
    message, payload = message_of(hidden, weight_ref[1], weights, sel_ref[...], 0.0)
    message_out[...] = message
    out_ref[...] = jnp.broadcast_to(payload[None], out_ref.shape)


def last_kernel(
    z_ref, mass_ref, atom_weight_ref, hidden_ref, message_ref, cols_ref, spread_ref, head_ref,
    potential_ref, scaled_ref,
):
    total = jnp.sum(z_ref[...].astype(F32), axis=0)
    hidden = updated(
        total[:WINDOW], mass_ref[:, 0:1], atom_weight_ref[1], hidden_ref[...], message_ref[...],
        spread_ref[...],
    )
    score = jnp.sum(hidden * head_ref[...], axis=1, keepdims=True)
    radius, weights = column(cols_ref[...], 0), column(cols_ref[...], 2)
    potential = radius * (1.0 + jnp.tanh(score))
    scaled = weights * potential
    lane = lax.broadcasted_iota(jnp.int32, (BLK, BLK), 1)
    flat = jnp.where(lane == 0, potential[:BLK], 0.0)
    flat = jnp.where(lane == 1, potential[BLK:], flat)
    flat = jnp.where(lane == 2, scaled[:BLK], flat)
    flat = jnp.where(lane == 3, scaled[BLK:], flat)
    flat = flat.T
    potential_ref[...] = flat[0:2]
    for k in range(scaled_ref.shape[0]):
        scaled_ref[k] = flat[2:4]


def fock_kernel(flipped_ref, psi_ref, scaled_ref, out_ref, weighted, scratch):
    side, _, width = out_ref.shape
    for k in range(side):
        scratch[2 * k : 2 * k + 2, :] = scaled_ref[k]
    tall = scratch[...].T
    for n in range(2 * side):
        rows = slice(n * BLK, (n + 1) * BLK)
        weighted[rows, :] = (tall[:, n : n + 1] * psi_ref[rows, :].astype(F32)).astype(BF16)
    for k in range(side):
        out_ref[k] = jnp.dot(
            flipped_ref[...], weighted[:, k * width : (k + 1) * width], preferred_element_type=F32
        ).astype(BF16)


def from_behind(value, axis):
    return [value] + [
        lax.ppermute(value, axis, [(i, (i + k) % SIDE) for i in range(SIDE)])
        for k in range(1, SIDE)
    ]


def across(value):
    groups = lax.axis_size(GRID)
    pairs = [(g, g + 1 if g % 2 else g - 1) for g in range(1, groups - 1)]
    return lax.ppermute(value, GRID, pairs)


def swap(value):
    return lax.ppermute(value, "c", [(0, 1), (1, 0)])


def exchange(parts, axes):
    return lax.all_to_all(parts, axes, split_axis=0, concat_axis=0, tiled=True)


def local(
    basis_values,
    block_lists,
    orbitals,
    point_weights,
    point_atoms,
    embed_scale,
    embed_shift,
    message_weight,
    atom_weight,
    head_weight,
):
    feat = embed_scale.shape[0]
    points = point_weights.shape[0]
    batches, batch_points, _ = basis_values.shape
    deep, width = orbitals.shape
    place = jnp.stack([lax.axis_index(a) for a in ("zl", "y", GRID, "c", "x")]).astype(jnp.int32)
    plane, column_size = lax.axis_size(PLANE), lax.axis_size(COLUMN)
    square_f32 = shape((points, feat), F32)

    outer = across(orbitals)
    parts = from_behind(basis_values, "zl")
    selector, spread, meta, window = call(
        prepare_kernel,
        (
            shape((ROWS, points), BF16),
            shape((points, BLK), BF16),
            shape((ROWS, feat), F32),
            shape((ROWS, width), BF16),
        ),
        2,
        scratch=[pltpu.VMEM((8, batch_points), F32)],
    )(point_atoms.reshape(batches, batch_points), point_weights.reshape(batches, batch_points))
    own = jnp.concatenate([orbitals, window], axis=0)
    rows = jnp.concatenate([own, outer, swap(own)], axis=0)
    gathered = exchange(jnp.broadcast_to(rows, (SIDE, *rows.shape)), ("y",))

    total_points = SIDE * points
    dense, flipped = call(
        spread_kernel,
        (shape((total_points, 3 * deep), BF16), shape((3 * deep, total_points), BF16)),
        2 + SIDE,
        smem=(0, 1),
    )(place, block_lists, *parts)
    psi, squares = call(
        psi_kernel,
        (
            shape((total_points, SIDE * width), BF16),
            shape((SIDE * SIDE, 4, batch_points), F32),
        ),
        3,
        smem=(0,),
        scratch=[pltpu.VMEM((total_points, BLK), F32)],
    )(place, dense, gathered)
    squares = exchange(squares, ("x", "zl"))
    radius = jnp.cbrt(jnp.sum(squares[:, :2], axis=0))

    weights = point_weights.reshape(batches, batch_points)
    to_plane = shape((plane, ROWS, feat), BF16)
    to_column = shape((column_size, ROWS, feat), BF16)
    tall = shape((batch_points, 8), F32)
    hidden, message, cols, sent = call(
        first_kernel,
        (square_f32, square_f32, tall, to_column),
        7,
        scratch=[pltpu.VMEM((8, batch_points), F32)],
    )(radius, weights, embed_scale[None], embed_shift[None], message_weight, selector, meta)
    sums, match = call(
        route_first_kernel,
        (to_plane, shape((column_size * ROWS, plane * WINDOW), BF16)),
        3,
        smem=(0,),
    )(place, exchange(sent, COLUMN), squares)
    hidden, message, mass_rows, sent = call(
        second_kernel, (square_f32, square_f32, shape((WINDOW, BLK), F32), to_column), 8
    )(
        exchange(sums, PLANE), atom_weight, message_weight, hidden, message, cols, spread, selector
    )
    sums = call(route_kernel, to_plane, 2)(exchange(sent, COLUMN), match)
    potential, scaled = call(
        last_kernel,
        (shape((batches, batch_points), F32), shape((SIDE, batches, batch_points), F32)),
        8,
    )(
        exchange(sums, PLANE), mass_rows, atom_weight, hidden, message, cols, spread,
        head_weight[None],
    )
    scaled = exchange(scaled, ("zl",))

    terms = call(
        fock_kernel,
        shape((SIDE, 3 * deep, width), BF16),
        3,
        scratch=[
            pltpu.VMEM((total_points, SIDE * width), BF16),
            pltpu.VMEM((8, batch_points), F32),
        ],
    )(flipped, psi, scaled)
    total = jnp.sum(exchange(terms, ("y",)).astype(F32), axis=0)
    own, outer, partner = total[:deep], total[deep : 2 * deep], total[2 * deep :]
    arrived = across(outer.astype(BF16))
    fock = own + arrived.astype(F32) + swap(partner.astype(BF16)).astype(F32)
    return fock, potential.reshape(-1)


def solution(mesh):
    finer = Mesh(mesh.devices.reshape(4, 4, 2, 4, 4), AXES)
    atom = ("zl", "y")
    placed = (
        P(AXES, None, None),
        P(GRID, None),
        P(GRID, atom),
        P(AXES),
        P(AXES),
        P(),
        P(),
        P(),
        P(),
        P(),
    )
    return jax.shard_map(
        local,
        mesh=finer,
        in_specs=placed,
        out_specs=(P(GRID, atom), P(AXES)),
        check_vma=False,
    )
```

```python
import jax
import jax.numpy as jnp
from jax import lax
from jax.experimental import pallas as pl
from jax.experimental.pallas import tpu as pltpu
from jax.sharding import Mesh
from jax.sharding import PartitionSpec as P

AXES = ("x", "zh", "c", "zl", "y")
GRID = ("x", "zh", "c")
PLANE = ("x", "c", "y")
COLUMN = ("zh", "zl")
SIDE = 4
BLK = 128
WINDOW = 8
NATOM = 512
ROWS = 16
F32 = jnp.float32
BF16 = jnp.bfloat16

VMEM = 16 * 1024 * 1024


def call(kernel, out_shape, n_in, smem=(), scratch=(), **kw):
    specs = [
        pl.BlockSpec(memory_space=pltpu.SMEM if i in smem else pltpu.VMEM) for i in range(n_in)
    ]
    outs = jax.tree.map(lambda _: pl.BlockSpec(memory_space=pltpu.VMEM), out_shape)
    return pl.pallas_call(
        kernel,
        out_shape=out_shape,
        in_specs=specs,
        out_specs=outs,
        scratch_shapes=list(scratch),
        compiler_params=pltpu.CompilerParams(vmem_limit_bytes=VMEM),
        **kw,
    )


def shape(dims, dtype):
    return jax.ShapeDtypeStruct(dims, dtype)


def prepare_kernel(atoms_ref, weights_ref, sel_ref, spread_ref, meta_ref, window_ref, scratch):
    atoms = atoms_ref[...].astype(F32)
    half = NATOM // 2
    first = atoms[0:1, 0:1]
    apart = atoms - first
    apart = jnp.where(apart < -half, apart + NATOM, jnp.where(apart >= half, apart - NATOM, apart))
    start = first + jnp.min(jnp.min(apart, axis=1, keepdims=True), axis=0, keepdims=True)
    start = jnp.where(start < 0, start + NATOM, jnp.where(start >= NATOM, start - NATOM, start))
    slot = atoms - start
    slot = jnp.where(slot < 0, slot + NATOM, slot)
    points = 2 * BLK
    wide = jnp.concatenate([slot[0:1], slot[1:2]], axis=1)
    weights = jnp.concatenate([weights_ref[0:1], weights_ref[1:2]], axis=1)
    rows = lax.broadcasted_iota(jnp.int32, (ROWS, points), 0).astype(F32)
    chosen = rows == wide
    sel_ref[...] = jnp.where(chosen, 1.0, 0.0).astype(BF16)
    scratch[...] = jnp.zeros_like(scratch)
    scratch[0:2, :] = slot
    tall = scratch[...].T
    lanes = lax.broadcasted_iota(jnp.int32, (points, BLK), 1).astype(F32)
    spread_ref[...] = jnp.where(lanes == column(tall, 0), 1.0, 0.0).astype(BF16)
    mass = jnp.sum(jnp.where(chosen, weights, 0.0), axis=1, keepdims=True)[:WINDOW]
    atom = start + lax.broadcasted_iota(jnp.int32, (WINDOW, 1), 0).astype(F32)
    atom = jnp.where(atom >= NATOM, atom - NATOM, atom)
    high = jnp.floor(atom * (1.0 / 16.0))
    low = atom - 16.0 * high
    lane = lax.broadcasted_iota(jnp.int32, (WINDOW, points), 1)
    facts = jnp.where(lane == 0, mass, jnp.where(lane == 1, high, jnp.where(lane == 2, low, 0.0)))
    meta_ref[...] = jnp.concatenate([jnp.zeros_like(facts), facts], axis=0)
    row = lax.broadcasted_iota(jnp.int32, window_ref.shape, 0)
    window_ref[...] = jnp.where(
        row == 0, high[0:1], jnp.where(row == 1, low[0:1], 0.0)
    ).astype(BF16)


def psi_kernel(place_ref, list_ref, parts_hbm, near_hbm, *refs):
    outer = refs[:SIDE]
    psi_ref, dens_ref, flipped_out, dense_ref, flipped_ref, acc_ref, *refs = refs[SIDE:]
    parts_ref, near_ref, sems = refs
    side = parts_ref.shape[0]
    part_copies = [
        pltpu.make_async_copy(parts_hbm.at[k], parts_ref.at[k], sems.at[k]) for k in range(side)
    ]
    near_copy = pltpu.make_async_copy(near_hbm, near_ref, sems.at[side])
    for copy in part_copies:
        copy.start()
    near_copy.start()
    _, y, group, core, x = (place_ref[i] for i in range(5))
    dense_ref[...] = jnp.zeros_like(dense_ref)
    flipped_ref[...] = jnp.zeros_like(flipped_ref)
    _, per, _, wide = parts_ref.shape
    deep, width = outer[0].shape
    owned = deep // BLK
    for k in range(side):
        part_copies[k].wait()
        for r in range(per):
            batch = (k * side + y) * per + r
            row = (k * per + r) * BLK
            for j in range(wide // BLK):
                block = list_ref[batch, j] - (group - 1) * owned
                below, above = block < owned, block >= 2 * owned
                within = jnp.where(below, block, jnp.where(above, block - 2 * owned, block - owned))
                far = jnp.where(below == (core == 0), 2, 1)
                third = jnp.where(jnp.logical_or(below, above), far, 0)
                col = pl.multiple_of((third * owned + within) * BLK, BLK)
                tile = parts_ref[k, r, :, j * BLK : (j + 1) * BLK]
                dense_ref[row : row + BLK, pl.ds(col, BLK)] = tile
                flipped_ref[pl.ds(col, BLK), row : row + BLK] = tile.T
    copy = pltpu.make_async_copy(flipped_ref, flipped_out, sems.at[side + 1])
    copy.start()
    near_copy.wait()
    lane = lax.broadcasted_iota(jnp.int32, (1, BLK), 1)
    device = lane // WINDOW
    atoms = (lane % WINDOW).astype(F32)
    for k in range(side):
        at = lax.rem(y - k + side, side)
        own, partner = core * side + at, (1 - core) * side + at
        chosen = jnp.concatenate(
            [near_ref[own, :deep], near_ref[partner, :deep], outer[k][...]], axis=0
        )
        psi = jnp.dot(dense_ref[...], chosen, preferred_element_type=F32).astype(BF16)
        psi_ref[:, k * width : (k + 1) * width] = psi
        wide = psi.astype(F32)
        square = wide * wide
        part = square[:, :BLK] + square[:, BLK:]
        if k == 0:
            acc_ref[...] = part
        else:
            acc_ref[...] += part
    for n in range(2 * side):
        window = near_ref[n, deep:, :BLK].astype(F32)
        window = window[0:1] * 16.0 + window[1:2]
        atoms += jnp.where(device == n, window, 0.0)
    atoms = jnp.where(atoms >= NATOM, atoms - NATOM, atoms)
    atoms = jnp.where(device < 2 * side, atoms, 0.0)
    dens_ref[...] = jnp.zeros_like(dens_ref)
    for n in range(dens_ref.shape[0]):
        dens_ref[n, 2:3, :] = atoms
    for n in range(acc_ref.shape[0] // BLK):
        tile = acc_ref[n * BLK : (n + 1) * BLK, :].T
        row = 2.0 * jnp.sum(tile, axis=0, keepdims=True)
        dens_ref[x * side + n // 2, n % 2 : n % 2 + 1, :] = row
    copy.wait()


def silu(x):
    return x * jax.nn.sigmoid(x)


def column(tall, n):
    return jnp.concatenate([tall[:, n : n + 1], tall[:, n + 1 : n + 2]], axis=0)


def message_of(hidden, weight, weights_col, selector, meta):
    message = silu(jnp.dot(hidden.astype(BF16), weight, preferred_element_type=F32))
    weighted = (weights_col * message).astype(BF16)
    rows = jnp.dot(selector, weighted, preferred_element_type=F32)
    return message, rows + meta


def first_kernel(
    radius_ref, pw_ref, scale_ref, shift_ref, weight_ref, sel_ref, meta_ref,
    hidden_ref, message_ref, cols_ref, out_ref, scratch,
):
    scratch[...] = jnp.zeros_like(scratch)
    scratch[0:2, :] = radius_ref[...]
    scratch[2:4, :] = pw_ref[...]
    tall = scratch[...].T
    cols_ref[...] = tall
    radius, weights = column(tall, 0), column(tall, 2)
    hidden = silu(radius * scale_ref[...] + shift_ref[...])
    hidden_ref[...] = hidden
    message, payload = message_of(hidden, weight_ref[0], weights, sel_ref[...], meta_ref[...])
    message_ref[...] = message
    out_ref[...] = jnp.broadcast_to(payload.astype(BF16)[None], out_ref.shape)


def folded(rows):
    return jnp.concatenate([rows[..., :BLK], rows[..., BLK:]], axis=-2)


def unfolded(rows):
    return jnp.concatenate([rows[:WINDOW], rows[WINDOW:]], axis=1)


def route_first_kernel(place_ref, x_ref, target_ref, out_ref, match_ref):
    n = x_ref.shape[0] * ROWS
    zl = place_ref[0]
    half = [target_ref[k * SIDE + zl, 2:3, :] for k in range(SIDE)]
    targets = jnp.concatenate(
        [half[0] + pltpu.roll(half[1], BLK // 2, 1), half[2] + pltpu.roll(half[3], BLK // 2, 1)],
        axis=1,
    )
    x = x_ref[...].reshape(n, x_ref.shape[2])
    meta = x[:, :BLK].astype(F32)
    meta = jnp.concatenate([meta[WINDOW:], meta[:WINDOW]], axis=0)
    atom = meta[:, 1:2] * 16.0 + meta[:, 2:3]
    row = lax.broadcasted_iota(jnp.int32, (n, targets.shape[1]), 0)
    valid = lax.rem(row, ROWS) < WINDOW
    match = jnp.where(jnp.logical_and(atom == targets, valid), 1.0, 0.0).astype(BF16)
    match_ref[...] = match
    down = (((0,), (0,)), ((), ()))
    sums = lax.dot_general(match, x, down, preferred_element_type=F32)
    mass = lax.dot_general(match, meta.astype(BF16), down, preferred_element_type=F32)
    count = out_ref.shape[0]
    mass = jnp.concatenate([mass, jnp.zeros_like(mass)], axis=1)
    both = jnp.concatenate(
        [sums.reshape(count, WINDOW, -1), mass.reshape(count, WINDOW, -1)], axis=1
    )
    out_ref[...] = both.astype(BF16)


def route_kernel(x_ref, match_ref, out_ref):
    x = x_ref[...].reshape(x_ref.shape[0] * ROWS, x_ref.shape[2])
    wide = x.astype(F32)
    rest = jnp.concatenate([wide[WINDOW:], wide[:WINDOW]], axis=0).astype(BF16)
    down = (((0,), (0,)), ((), ()))
    halves = [
        lax.dot_general(match_ref[...], half, down, preferred_element_type=F32).reshape(
            out_ref.shape[0], WINDOW, -1
        )
        for half in (x, rest)
    ]
    out_ref[...] = jnp.concatenate(halves, axis=1).astype(BF16)


def updated(rows, mass, weight, hidden, message, spread):
    mean = rows / (1.0 + mass)
    mean = jnp.concatenate([mean, jnp.zeros_like(mean)], axis=0).astype(BF16)
    update = silu(jnp.dot(mean, weight, preferred_element_type=F32)).astype(BF16)
    filler = jnp.zeros((BLK - ROWS, update.shape[1]), BF16)
    update = jnp.concatenate([update, filler], axis=0)
    picked = jnp.dot(spread, update, preferred_element_type=F32)
    return hidden + message * picked


def second_kernel(
    z_ref, atom_weight_ref, weight_ref, hidden_ref, message_ref, cols_ref, spread_ref, sel_ref,
    hidden_out, message_out, mass_ref, out_ref,
):
    total = jnp.sum(z_ref[...].astype(F32), axis=0)
    mass = jnp.broadcast_to(total[WINDOW:, 0:1], mass_ref.shape)
    mass_ref[...] = mass
    hidden = updated(
        total[:WINDOW], mass[:, 0:1], atom_weight_ref[0], hidden_ref[...], message_ref[...],
        spread_ref[...],
    )
    hidden_out[...] = hidden
    weights = column(cols_ref[...], 2)
    message, payload = message_of(hidden, weight_ref[1], weights, sel_ref[...], 0.0)
    message_out[...] = message
    payload = folded(payload[:WINDOW]).astype(BF16)
    out_ref[...] = jnp.broadcast_to(payload[None], out_ref.shape)


def last_kernel(
    z_ref, mass_ref, atom_weight_ref, hidden_ref, message_ref, cols_ref, spread_ref, head_ref,
    potential_ref, scaled_ref,
):
    total = jnp.sum(z_ref[...].astype(F32), axis=0)
    hidden = updated(
        unfolded(total), mass_ref[:, 0:1], atom_weight_ref[1], hidden_ref[...], message_ref[...],
        spread_ref[...],
    )
    score = jnp.sum(hidden * head_ref[...], axis=1, keepdims=True)
    radius, weights = column(cols_ref[...], 0), column(cols_ref[...], 2)
    potential = radius * (1.0 + jnp.tanh(score))
    scaled = weights * potential
    lane = lax.broadcasted_iota(jnp.int32, (BLK, BLK), 1)
    flat = jnp.where(lane == 0, potential[:BLK], 0.0)
    flat = jnp.where(lane == 1, potential[BLK:], flat)
    flat = jnp.where(lane == 2, scaled[:BLK], flat)
    flat = jnp.where(lane == 3, scaled[BLK:], flat)
    flat = flat.T
    potential_ref[...] = flat[0:2]
    for k in range(scaled_ref.shape[0]):
        scaled_ref[k] = flat[2:4]


def scaled_psi(psi_ref, scaled_ref, weighted, scratch):
    side = scaled_ref.shape[0]
    for k in range(side):
        scratch[2 * k : 2 * k + 2, :] = scaled_ref[k]
    tall = scratch[...].T
    for n in range(2 * side):
        rows = slice(n * BLK, (n + 1) * BLK)
        weighted[rows, :] = (tall[:, n : n + 1] * psi_ref[rows, :].astype(F32)).astype(BF16)


def outer_kernel(
    place_ref, flipped_hbm, psi_ref, scaled_ref, out_ref, weighted, flipped_ref, scratch, sem
):
    side, deep, width = out_ref.shape
    copy = pltpu.make_async_copy(flipped_hbm.at[2 * deep :], flipped_ref, sem)
    copy.start()
    y = place_ref[1]
    scaled_psi(psi_ref, scaled_ref, weighted, scratch)
    copy.wait()
    for k in range(side):
        terms = jnp.dot(
            flipped_ref[...],
            weighted[:, k * width : (k + 1) * width],
            preferred_element_type=F32,
        )
        out_ref[lax.rem(y - k + side, side)] = terms.astype(BF16)


def near_kernel(
    place_ref, flipped_hbm, psi_ref, scaled_ref, out_ref, weighted, flipped_ref, scratch, sem
):
    count, deep, width = out_ref.shape
    side = count // 2
    copy = pltpu.make_async_copy(flipped_hbm.at[: 2 * deep], flipped_ref, sem)
    copy.start()
    y, core = place_ref[1], place_ref[3]
    scaled_psi(psi_ref, scaled_ref, weighted, scratch)
    copy.wait()
    for k in range(side):
        terms = jnp.dot(
            flipped_ref[...],
            weighted[:, k * width : (k + 1) * width],
            preferred_element_type=F32,
        ).astype(BF16)
        at = lax.rem(y - k + side, side)
        out_ref[core * side + at] = terms[:deep]
        out_ref[(1 - core) * side + at] = terms[deep:]


def from_behind(value, axis):
    return [value] + [
        lax.ppermute(value, axis, [(i, (i + k) % SIDE) for i in range(SIDE)])
        for k in range(1, SIDE)
    ]


def across(value):
    groups = lax.axis_size(GRID)
    pairs = [(g, g + 1 if g % 2 else g - 1) for g in range(1, groups - 1)]
    return lax.ppermute(value, GRID, pairs)


def exchange(parts, axes):
    return lax.all_to_all(parts, axes, split_axis=0, concat_axis=0, tiled=True)


def local(
    basis_values,
    block_lists,
    orbitals,
    point_weights,
    point_atoms,
    embed_scale,
    embed_shift,
    message_weight,
    atom_weight,
    head_weight,
):
    feat = embed_scale.shape[0]
    points = point_weights.shape[0]
    batches, batch_points, _ = basis_values.shape
    deep, width = orbitals.shape
    place = jnp.stack([lax.axis_index(a) for a in ("zl", "y", GRID, "c", "x")]).astype(jnp.int32)
    plane, column_size = lax.axis_size(PLANE), lax.axis_size(COLUMN)
    square_f32 = shape((points, feat), F32)

    parts = lax.all_gather(basis_values, "zl")
    outer = across(orbitals)
    selector, spread, meta, window = call(
        prepare_kernel,
        (
            shape((ROWS, points), BF16),
            shape((points, BLK), BF16),
            shape((ROWS, feat), F32),
            shape((ROWS, width), BF16),
        ),
        2,
        scratch=[pltpu.VMEM((8, batch_points), F32)],
    )(point_atoms.reshape(batches, batch_points), point_weights.reshape(batches, batch_points))
    own = jnp.concatenate([orbitals, window], axis=0)
    chip = ("c", "y")
    near = exchange(jnp.broadcast_to(own, (2 * SIDE, *own.shape)), chip)
    outer = from_behind(outer, "y")

    total_points = SIDE * points
    everywhere = pl.BlockSpec(memory_space=pltpu.VMEM)
    scalars = pl.BlockSpec(memory_space=pltpu.SMEM)
    anywhere = pl.BlockSpec(memory_space=pl.ANY)
    psi, squares, flipped = pl.pallas_call(
        psi_kernel,
        out_shape=(
            shape((total_points, SIDE * width), BF16),
            shape((SIDE * SIDE, 4, batch_points), F32),
            shape((3 * deep, total_points), BF16),
        ),
        in_specs=[scalars] * 2 + [anywhere] * 2 + [everywhere] * SIDE,
        out_specs=(everywhere, everywhere, anywhere),
        scratch_shapes=[
            pltpu.VMEM((total_points, 3 * deep), BF16),
            pltpu.VMEM((3 * deep, total_points), BF16),
            pltpu.VMEM((total_points, BLK), F32),
            pltpu.VMEM(parts.shape, BF16),
            pltpu.VMEM(near.shape, BF16),
            pltpu.SemaphoreType.DMA((SIDE + 2,)),
        ],
        compiler_params=pltpu.CompilerParams(vmem_limit_bytes=VMEM),
    )(place, block_lists, parts, near, *outer)
    squares = exchange(squares, ("x", "zl"))
    radius = jnp.cbrt(jnp.sum(squares[:, :2], axis=0))

    weights = point_weights.reshape(batches, batch_points)
    to_plane = shape((plane, ROWS, feat), BF16)
    to_column = shape((column_size, ROWS, feat), BF16)
    tall = shape((batch_points, 8), F32)
    hidden, message, cols, sent = call(
        first_kernel,
        (square_f32, square_f32, tall, to_column),
        7,
        scratch=[pltpu.VMEM((8, batch_points), F32)],
    )(radius, weights, embed_scale[None], embed_shift[None], message_weight, selector, meta)
    sums, match = call(
        route_first_kernel,
        (to_plane, shape((column_size * ROWS, plane * WINDOW), BF16)),
        3,
        smem=(0,),
    )(place, exchange(sent, COLUMN), squares)
    hidden, message, mass_rows, sent = call(
        second_kernel,
        (
            square_f32,
            square_f32,
            shape((WINDOW, BLK), F32),
            shape((column_size, ROWS, BLK), BF16),
        ),
        8,
    )(
        exchange(sums, PLANE), atom_weight, message_weight, hidden, message, cols, spread, selector
    )
    sums = call(route_kernel, shape((plane, ROWS, BLK), BF16), 2)(exchange(sent, COLUMN), match)
    potential, scaled = call(
        last_kernel,
        (shape((batches, batch_points), F32), shape((SIDE, batches, batch_points), F32)),
        8,
    )(
        exchange(sums, PLANE), mass_rows, atom_weight, hidden, message, cols, spread,
        head_weight[None],
    )
    scaled = exchange(scaled, ("zl",))

    def fock_terms(kernel, devices, rows):
        return pl.pallas_call(
            kernel,
            out_shape=shape((devices, deep, width), BF16),
            in_specs=[scalars, anywhere, everywhere, everywhere],
            out_specs=everywhere,
            scratch_shapes=[
                pltpu.VMEM((total_points, SIDE * width), BF16),
                pltpu.VMEM((rows, total_points), BF16),
                pltpu.VMEM((8, batch_points), F32),
                pltpu.SemaphoreType.DMA,
            ],
            compiler_params=pltpu.CompilerParams(vmem_limit_bytes=VMEM),
        )(place, flipped, psi, scaled)

    outer = fock_terms(outer_kernel, SIDE, deep)
    near = fock_terms(near_kernel, 2 * SIDE, 2 * deep)
    arrived = across(jnp.sum(exchange(outer, ("y",)).astype(F32), axis=0).astype(BF16))
    fock = jnp.sum(exchange(near, chip).astype(F32), axis=0) + arrived.astype(F32)
    return fock, potential.reshape(-1)


def solution(mesh):
    finer = Mesh(mesh.devices.reshape(4, 4, 2, 4, 4), AXES)
    atom = ("zl", "y")
    placed = (
        P(AXES, None, None),
        P(GRID, None),
        P(GRID, atom),
        P(AXES),
        P(AXES),
        P(),
        P(),
        P(),
        P(),
        P(),
    )
    return jax.shard_map(
        local,
        mesh=finer,
        in_specs=placed,
        out_specs=(P(GRID, atom), P(AXES)),
        check_vma=False,
    )
```

```python
import jax
import jax.numpy as jnp
from jax import lax
from jax.experimental import pallas as pl
from jax.experimental.pallas import tpu as pltpu
from jax.sharding import Mesh
from jax.sharding import PartitionSpec as P

AXES = ("x", "zh", "c", "zl", "y")
GRID = ("x", "zh", "c")
PLANE = ("x", "c", "y")
COLUMN = ("zh", "zl")
SIDE = 4
BLK = 128
WINDOW = 8
NATOM = 512
ROWS = 16
SPARE = 16
F32 = jnp.float32
BF16 = jnp.bfloat16

VMEM = 16 * 1024 * 1024


def call(kernel, out_shape, n_in, smem=(), scratch=(), **kw):
    specs = [
        pl.BlockSpec(memory_space=pltpu.SMEM if i in smem else pltpu.VMEM) for i in range(n_in)
    ]
    outs = jax.tree.map(lambda _: pl.BlockSpec(memory_space=pltpu.VMEM), out_shape)
    return pl.pallas_call(
        kernel,
        out_shape=out_shape,
        in_specs=specs,
        out_specs=outs,
        scratch_shapes=list(scratch),
        compiler_params=pltpu.CompilerParams(vmem_limit_bytes=VMEM),
        **kw,
    )


def shape(dims, dtype):
    return jax.ShapeDtypeStruct(dims, dtype)


def prepare_kernel(atoms_ref, weights_ref, sel_ref, spread_ref, meta_ref, window_ref, scratch):
    atoms = atoms_ref[...].astype(F32)
    half = NATOM // 2
    first = atoms[0:1, 0:1]
    apart = atoms - first
    apart = jnp.where(apart < -half, apart + NATOM, jnp.where(apart >= half, apart - NATOM, apart))
    start = first + jnp.min(jnp.min(apart, axis=1, keepdims=True), axis=0, keepdims=True)
    start = jnp.where(start < 0, start + NATOM, jnp.where(start >= NATOM, start - NATOM, start))
    slot = atoms - start
    slot = jnp.where(slot < 0, slot + NATOM, slot)
    points = 2 * BLK
    wide = jnp.concatenate([slot[0:1], slot[1:2]], axis=1)
    weights = jnp.concatenate([weights_ref[0:1], weights_ref[1:2]], axis=1)
    rows = lax.broadcasted_iota(jnp.int32, (ROWS, points), 0).astype(F32)
    chosen = rows == wide
    sel_ref[...] = jnp.where(chosen, 1.0, 0.0).astype(BF16)
    scratch[...] = jnp.zeros_like(scratch)
    scratch[0:2, :] = slot
    tall = scratch[...].T
    lanes = lax.broadcasted_iota(jnp.int32, (points, BLK), 1).astype(F32)
    spread_ref[...] = jnp.where(lanes == column(tall, 0), 1.0, 0.0).astype(BF16)
    mass = jnp.sum(jnp.where(chosen, weights, 0.0), axis=1, keepdims=True)[:WINDOW]
    atom = start + lax.broadcasted_iota(jnp.int32, (WINDOW, 1), 0).astype(F32)
    atom = jnp.where(atom >= NATOM, atom - NATOM, atom)
    high = jnp.floor(atom * (1.0 / 16.0))
    low = atom - 16.0 * high
    lane = lax.broadcasted_iota(jnp.int32, (WINDOW, points), 1)
    facts = jnp.where(lane == 0, mass, jnp.where(lane == 1, high, jnp.where(lane == 2, low, 0.0)))
    meta_ref[...] = jnp.concatenate([jnp.zeros_like(facts), facts], axis=0)
    row = lax.broadcasted_iota(jnp.int32, (ROWS, BLK), 0)
    window = jnp.where(row == 0, high[0:1], jnp.where(row == 1, low[0:1], 0.0)).astype(BF16)
    window_ref[...] = jnp.broadcast_to(window[None], window_ref.shape)


def rows_kernel(own_ref, outer_ref, windows_ref, out_ref):
    deep, width = own_ref.shape
    lane = lax.broadcasted_iota(jnp.int32, (ROWS, width), 1)
    windows = jnp.zeros((ROWS, width), F32)
    for n in range(windows_ref.shape[0]):
        windows = jnp.where(lane == n, windows_ref[n, :, 0:1].astype(F32), windows)
    windows = windows.astype(BF16)
    for k in range(out_ref.shape[0]):
        out_ref[k, :deep] = own_ref[...]
        out_ref[k, deep : 2 * deep] = outer_ref[...]
        out_ref[k, 2 * deep :] = windows


def psi_kernel(place_ref, list_ref, near_ref, partner_ref, *refs):
    parts = refs[:SIDE]
    psi_ref, dens_ref, target_ref, flipped_hbm, dense_ref, flipped_ref, acc_ref, sem = refs[SIDE:]
    side = len(parts)
    per, _, wide = parts[0].shape
    zl, y, group, core = (place_ref[i] for i in range(4))
    dense_ref[...] = jnp.zeros_like(dense_ref)
    flipped_ref[...] = jnp.zeros_like(flipped_ref)
    _, deep, width = partner_ref.shape
    owned = deep // BLK
    lane = lax.broadcasted_iota(jnp.int32, target_ref.shape, 1)
    device = lane // WINDOW
    atoms = (lane % WINDOW).astype(F32)
    for k in range(side):
        window = near_ref[k, 2 * deep :, :BLK].astype(F32)
        window = window[0:1] * 16.0 + window[1:2]
        for n in range(2 * side):
            atoms += jnp.where(device == n * side + k, window[:, n : n + 1], 0.0)
    target_ref[...] = jnp.where(atoms >= NATOM, atoms - NATOM, atoms)
    for k, part in enumerate(parts):
        origin = lax.rem(zl - k + side, side)
        for r in range(per):
            batch = (origin * side + y) * per + r
            row = pl.multiple_of((origin * per + r) * BLK, BLK)
            for j in range(wide // BLK):
                block = list_ref[batch, j] - (group - 1) * owned
                below, above = block < owned, block >= 2 * owned
                within = jnp.where(below, block, jnp.where(above, block - 2 * owned, block - owned))
                far = jnp.where(below == (core == 0), 2, 1)
                third = jnp.where(jnp.logical_or(below, above), far, 0)
                col = pl.multiple_of((third * owned + within) * BLK, BLK)
                tile = part[r, :, j * BLK : (j + 1) * BLK]
                dense_ref[pl.ds(row, BLK), pl.ds(col, BLK)] = tile
                flipped_ref[pl.ds(col, BLK), pl.ds(row, BLK)] = tile.T
    copy = pltpu.make_async_copy(flipped_ref, flipped_hbm.at[0], sem)
    copy.start()
    for k in range(side):
        chosen = jnp.concatenate(
            [near_ref[k, :deep], partner_ref[k], near_ref[k, deep : 2 * deep]], axis=0
        )
        psi = jnp.dot(dense_ref[...], chosen, preferred_element_type=F32).astype(BF16)
        psi_ref[:, k * width : (k + 1) * width] = psi
        wide_psi = psi.astype(F32)
        square = wide_psi * wide_psi
        part = square[:, :BLK] + square[:, BLK:]
        if k == 0:
            acc_ref[...] = part
        else:
            acc_ref[...] += part
    for n in range(acc_ref.shape[0] // BLK):
        tile = acc_ref[n * BLK : (n + 1) * BLK, :].T
        dens_ref[n // 2, n % 2 : n % 2 + 1, :] = 2.0 * jnp.sum(tile, axis=0, keepdims=True)
    copy.wait()


def silu(x):
    return x * jax.nn.sigmoid(x)


def column(tall, n):
    return jnp.concatenate([tall[:, n : n + 1], tall[:, n + 1 : n + 2]], axis=0)


def message_of(hidden, weight, weights_col, selector, meta):
    message = silu(jnp.dot(hidden.astype(BF16), weight, preferred_element_type=F32))
    weighted = (weights_col * message).astype(BF16)
    rows = jnp.dot(selector, weighted, preferred_element_type=F32)
    return message, rows + meta


def first_kernel(
    radius_ref, pw_ref, scale_ref, shift_ref, weight_ref, sel_ref, meta_ref,
    hidden_ref, message_ref, cols_ref, out_ref, scratch,
):
    scratch[...] = jnp.zeros_like(scratch)
    scratch[0:2, :] = radius_ref[...]
    scratch[2:4, :] = pw_ref[...]
    tall = scratch[...].T
    cols_ref[...] = tall
    radius, weights = column(tall, 0), column(tall, 2)
    hidden = silu(radius * scale_ref[...] + shift_ref[...])
    hidden_ref[...] = hidden
    message, payload = message_of(hidden, weight_ref[0], weights, sel_ref[...], meta_ref[...])
    message_ref[...] = message
    out_ref[...] = jnp.broadcast_to(payload.astype(BF16)[None], out_ref.shape)


def folded(rows):
    return jnp.concatenate([rows[..., :BLK], rows[..., BLK:]], axis=-2)


def unfolded(rows):
    return jnp.concatenate([rows[:WINDOW], rows[WINDOW:]], axis=1)


def route_first_kernel(x_ref, target_ref, out_ref, match_ref):
    n = x_ref.shape[0] * ROWS
    targets = target_ref[...]
    x = x_ref[...].reshape(n, x_ref.shape[2])
    meta = x[:, :BLK].astype(F32)
    meta = jnp.concatenate([meta[WINDOW:], meta[:WINDOW]], axis=0)
    atom = meta[:, 1:2] * 16.0 + meta[:, 2:3]
    row = lax.broadcasted_iota(jnp.int32, (n, targets.shape[1]), 0)
    valid = lax.rem(row, ROWS) < WINDOW
    match = jnp.where(jnp.logical_and(atom == targets, valid), 1.0, 0.0).astype(BF16)
    match_ref[...] = match
    down = (((0,), (0,)), ((), ()))
    sums = lax.dot_general(match, x, down, preferred_element_type=F32)
    mass = lax.dot_general(match, meta.astype(BF16), down, preferred_element_type=F32)
    count = out_ref.shape[0]
    mass = jnp.concatenate([mass, jnp.zeros_like(mass)], axis=1)
    both = jnp.concatenate(
        [sums.reshape(count, WINDOW, -1), mass.reshape(count, WINDOW, -1)], axis=1
    )
    out_ref[...] = both.astype(BF16)


def route_kernel(x_ref, match_ref, out_ref):
    x = x_ref[...].reshape(x_ref.shape[0] * ROWS, x_ref.shape[2])
    wide = x.astype(F32)
    rest = jnp.concatenate([wide[WINDOW:], wide[:WINDOW]], axis=0).astype(BF16)
    down = (((0,), (0,)), ((), ()))
    halves = [
        lax.dot_general(match_ref[...], half, down, preferred_element_type=F32).reshape(
            out_ref.shape[0], WINDOW, -1
        )
        for half in (x, rest)
    ]
    out_ref[...] = jnp.concatenate(halves, axis=1).astype(BF16)


def updated(rows, mass, weight, hidden, message, spread):
    mean = rows / (1.0 + mass)
    mean = jnp.concatenate([mean, jnp.zeros_like(mean)], axis=0).astype(BF16)
    update = silu(jnp.dot(mean, weight, preferred_element_type=F32)).astype(BF16)
    filler = jnp.zeros((BLK - ROWS, update.shape[1]), BF16)
    update = jnp.concatenate([update, filler], axis=0)
    picked = jnp.dot(spread, update, preferred_element_type=F32)
    return hidden + message * picked


def second_kernel(
    z_ref, atom_weight_ref, weight_ref, hidden_ref, message_ref, cols_ref, spread_ref, sel_ref,
    hidden_out, message_out, mass_ref, out_ref,
):
    total = jnp.sum(z_ref[...].astype(F32), axis=0)
    mass = jnp.broadcast_to(total[WINDOW:, 0:1], mass_ref.shape)
    mass_ref[...] = mass
    hidden = updated(
        total[:WINDOW], mass[:, 0:1], atom_weight_ref[0], hidden_ref[...], message_ref[...],
        spread_ref[...],
    )
    hidden_out[...] = hidden
    weights = column(cols_ref[...], 2)
    message, payload = message_of(hidden, weight_ref[1], weights, sel_ref[...], 0.0)
    message_out[...] = message
    payload = folded(payload[:WINDOW]).astype(BF16)
    out_ref[...] = jnp.broadcast_to(payload[None], out_ref.shape)


def last_kernel(
    z_ref, mass_ref, atom_weight_ref, hidden_ref, message_ref, cols_ref, spread_ref, head_ref,
    potential_ref, scaled_ref,
):
    total = jnp.sum(z_ref[...].astype(F32), axis=0)
    hidden = updated(
        unfolded(total), mass_ref[:, 0:1], atom_weight_ref[1], hidden_ref[...], message_ref[...],
        spread_ref[...],
    )
    score = jnp.sum(hidden * head_ref[...], axis=1, keepdims=True)
    radius, weights = column(cols_ref[...], 0), column(cols_ref[...], 2)
    potential = radius * (1.0 + jnp.tanh(score))
    scaled = weights * potential
    lane = lax.broadcasted_iota(jnp.int32, (BLK, BLK), 1)
    flat = jnp.where(lane == 0, potential[:BLK], 0.0)
    flat = jnp.where(lane == 1, potential[BLK:], flat)
    flat = jnp.where(lane == 2, scaled[:BLK], flat)
    flat = jnp.where(lane == 3, scaled[BLK:], flat)
    flat = flat.T
    potential_ref[...] = flat[0:2]
    for k in range(scaled_ref.shape[0]):
        scaled_ref[k] = flat[2:4]


def scaled_psi(psi_ref, scaled_ref, weighted, scratch):
    side = scaled_ref.shape[0]
    for k in range(side):
        scratch[2 * k : 2 * k + 2, :] = scaled_ref[k]
    tall = scratch[...].T
    for n in range(2 * side):
        rows = slice(n * BLK, (n + 1) * BLK)
        weighted[rows, :] = (tall[:, n : n + 1] * psi_ref[rows, :].astype(F32)).astype(BF16)


def outer_kernel(
    place_ref, flipped_hbm, psi_ref, scaled_ref, out_ref, weighted, flipped_ref, scratch, sem
):
    side, deep, width = out_ref.shape
    copy = pltpu.make_async_copy(flipped_hbm.at[0, 2 * deep :], flipped_ref, sem)
    copy.start()
    scaled_psi(psi_ref, scaled_ref, weighted, scratch)
    copy.wait()
    for k in range(side):
        terms = jnp.dot(
            flipped_ref[...],
            weighted[:, k * width : (k + 1) * width],
            preferred_element_type=F32,
        )
        out_ref[k] = terms.astype(BF16)


def near_kernel(
    place_ref, flipped_hbm, psi_ref, scaled_ref, out_ref, weighted, flipped_ref, scratch, sem
):
    count, deep, width = out_ref.shape
    side = count // 2
    copy = pltpu.make_async_copy(flipped_hbm.at[0, : 2 * deep], flipped_ref, sem)
    copy.start()
    core = place_ref[3]
    scaled_psi(psi_ref, scaled_ref, weighted, scratch)
    copy.wait()
    for k in range(side):
        terms = jnp.dot(
            flipped_ref[...],
            weighted[:, k * width : (k + 1) * width],
            preferred_element_type=F32,
        ).astype(BF16)
        out_ref[core * side + k] = terms[:deep]
        out_ref[(1 - core) * side + k] = terms[deep:]


def from_behind(value, axis):
    return [value] + [
        lax.ppermute(value, axis, [(i, (i + k) % SIDE) for i in range(SIDE)])
        for k in range(1, SIDE)
    ]


def across(value):
    groups = lax.axis_size(GRID)
    pairs = [(g, g + 1 if g % 2 else g - 1) for g in range(1, groups - 1)]
    return lax.ppermute(value, GRID, pairs)


def swap(value):
    return lax.ppermute(value, "c", [(0, 1), (1, 0)])


def exchange(parts, axes):
    return lax.all_to_all(parts, axes, split_axis=0, concat_axis=0, tiled=True)


def local(
    basis_values,
    block_lists,
    orbitals,
    point_weights,
    point_atoms,
    embed_scale,
    embed_shift,
    message_weight,
    atom_weight,
    head_weight,
):
    feat = embed_scale.shape[0]
    points = point_weights.shape[0]
    batches, batch_points, _ = basis_values.shape
    deep, width = orbitals.shape
    place = jnp.stack([lax.axis_index(a) for a in ("zl", "y", GRID, "c")]).astype(jnp.int32)
    plane, column_size = lax.axis_size(PLANE), lax.axis_size(COLUMN)
    square_f32 = shape((points, feat), F32)

    outer = across(orbitals)
    selector, spread, meta, window = call(
        prepare_kernel,
        (
            shape((ROWS, points), BF16),
            shape((points, BLK), BF16),
            shape((ROWS, feat), F32),
            shape((2 * SIDE, ROWS, BLK), BF16),
        ),
        2,
        scratch=[pltpu.VMEM((8, batch_points), F32)],
    )(point_atoms.reshape(batches, batch_points), point_weights.reshape(batches, batch_points))
    windows = exchange(window, ("x", "c"))
    rows = call(rows_kernel, shape((SIDE, 2 * deep + ROWS, width), BF16), 3)(
        orbitals, outer, windows
    )
    near = exchange(rows, ("y",))
    near, *parts = lax.optimization_barrier((near, *from_behind(basis_values, "zl")))
    partner = swap(near[:, :deep])

    total_points = SIDE * points
    everywhere = pl.BlockSpec(memory_space=pltpu.VMEM)
    scalars = pl.BlockSpec(memory_space=pltpu.SMEM)
    anywhere = pl.BlockSpec(memory_space=pl.ANY)
    psi, squares, targets, flipped = pl.pallas_call(
        psi_kernel,
        out_shape=(
            shape((total_points, SIDE * width), BF16),
            shape((SIDE, batches, batch_points), F32),
            shape((1, plane * WINDOW), F32),
            shape((SPARE, 3 * deep, total_points), BF16),
        ),
        in_specs=[scalars] * 2 + [everywhere] * (2 + SIDE),
        out_specs=(everywhere, everywhere, everywhere, anywhere),
        scratch_shapes=[
            pltpu.VMEM((total_points, 3 * deep), BF16),
            pltpu.VMEM((3 * deep, total_points), BF16),
            pltpu.VMEM((total_points, BLK), F32),
            pltpu.SemaphoreType.DMA,
        ],
        compiler_params=pltpu.CompilerParams(vmem_limit_bytes=VMEM),
    )(place, block_lists, near, partner, *parts)
    squares = exchange(squares, ("zl",))
    radius = jnp.cbrt(jnp.sum(squares, axis=0))

    weights = point_weights.reshape(batches, batch_points)
    to_plane = shape((plane, ROWS, feat), BF16)
    to_column = shape((column_size, ROWS, feat), BF16)
    tall = shape((batch_points, 8), F32)
    hidden, message, cols, sent = call(
        first_kernel,
        (square_f32, square_f32, tall, to_column),
        7,
        scratch=[pltpu.VMEM((8, batch_points), F32)],
    )(radius, weights, embed_scale[None], embed_shift[None], message_weight, selector, meta)
    sums, match = call(
        route_first_kernel,
        (to_plane, shape((column_size * ROWS, plane * WINDOW), BF16)),
        2,
    )(exchange(sent, COLUMN), targets)
    hidden, message, mass_rows, sent = call(
        second_kernel,
        (
            square_f32,
            square_f32,
            shape((WINDOW, BLK), F32),
            shape((column_size, ROWS, BLK), BF16),
        ),
        8,
    )(
        exchange(sums, PLANE), atom_weight, message_weight, hidden, message, cols, spread, selector
    )
    sums = call(route_kernel, shape((plane, ROWS, BLK), BF16), 2)(exchange(sent, COLUMN), match)
    potential, scaled = call(
        last_kernel,
        (shape((batches, batch_points), F32), shape((SIDE, batches, batch_points), F32)),
        8,
    )(
        exchange(sums, PLANE), mass_rows, atom_weight, hidden, message, cols, spread,
        head_weight[None],
    )
    scaled = exchange(scaled, ("zl",))

    def fock_terms(kernel, devices, rows):
        return pl.pallas_call(
            kernel,
            out_shape=shape((devices, deep, width), BF16),
            in_specs=[scalars, anywhere, everywhere, everywhere],
            out_specs=everywhere,
            scratch_shapes=[
                pltpu.VMEM((total_points, SIDE * width), BF16),
                pltpu.VMEM((rows, total_points), BF16),
                pltpu.VMEM((8, batch_points), F32),
                pltpu.SemaphoreType.DMA,
            ],
            compiler_params=pltpu.CompilerParams(vmem_limit_bytes=VMEM),
        )(place, flipped, psi, scaled)

    outer = fock_terms(outer_kernel, SIDE, deep)
    near = fock_terms(near_kernel, 2 * SIDE, 2 * deep)
    arrived = across(jnp.sum(exchange(outer, ("y",)).astype(F32), axis=0).astype(BF16))
    fock = jnp.sum(exchange(near, ("c", "y")).astype(F32), axis=0) + arrived.astype(F32)
    return fock, potential.reshape(-1)


def solution(mesh):
    finer = Mesh(mesh.devices.reshape(4, 4, 2, 4, 4), AXES)
    atom = ("zl", "y")
    placed = (
        P(AXES, None, None),
        P(GRID, None),
        P(GRID, atom),
        P(AXES),
        P(AXES),
        P(),
        P(),
        P(),
        P(),
        P(),
    )
    return jax.shard_map(
        local,
        mesh=finer,
        in_specs=placed,
        out_specs=(P(GRID, atom), P(AXES)),
        check_vma=False,
    )
```

```python
import jax
import jax.numpy as jnp
from jax import lax
from jax.experimental import pallas as pl
from jax.experimental.pallas import tpu as pltpu
from jax.sharding import Mesh
from jax.sharding import PartitionSpec as P

AXES = ("x", "zh", "c", "zl", "y")
GRID = ("x", "zh", "c")
PLANE = ("x", "c", "y")
COLUMN = ("zh", "zl")
SIDE = 4
BLK = 128
WINDOW = 8
NATOM = 512
ROWS = 16
SPARE = 24
F32 = jnp.float32
BF16 = jnp.bfloat16

VMEM = 16 * 1024 * 1024


def call(kernel, out_shape, n_in, smem=(), scratch=(), **kw):
    specs = [
        pl.BlockSpec(memory_space=pltpu.SMEM if i in smem else pltpu.VMEM) for i in range(n_in)
    ]
    outs = jax.tree.map(lambda _: pl.BlockSpec(memory_space=pltpu.VMEM), out_shape)
    return pl.pallas_call(
        kernel,
        out_shape=out_shape,
        in_specs=specs,
        out_specs=outs,
        scratch_shapes=list(scratch),
        compiler_params=pltpu.CompilerParams(vmem_limit_bytes=VMEM),
        **kw,
    )


def shape(dims, dtype):
    return jax.ShapeDtypeStruct(dims, dtype)


def prepare_kernel(atoms_ref, weights_ref, sel_ref, spread_ref, meta_ref, window_ref, scratch):
    atoms = atoms_ref[...].astype(F32)
    half = NATOM // 2
    first = atoms[0:1, 0:1]
    apart = atoms - first
    apart = jnp.where(apart < -half, apart + NATOM, jnp.where(apart >= half, apart - NATOM, apart))
    start = first + jnp.min(jnp.min(apart, axis=1, keepdims=True), axis=0, keepdims=True)
    start = jnp.where(start < 0, start + NATOM, jnp.where(start >= NATOM, start - NATOM, start))
    slot = atoms - start
    slot = jnp.where(slot < 0, slot + NATOM, slot)
    points = 2 * BLK
    wide = jnp.concatenate([slot[0:1], slot[1:2]], axis=1)
    weights = jnp.concatenate([weights_ref[0:1], weights_ref[1:2]], axis=1)
    rows = lax.broadcasted_iota(jnp.int32, (ROWS, points), 0).astype(F32)
    chosen = rows == wide
    sel_ref[...] = jnp.where(chosen, 1.0, 0.0).astype(BF16)
    scratch[...] = jnp.zeros_like(scratch)
    scratch[0:2, :] = slot
    tall = scratch[...].T
    lanes = lax.broadcasted_iota(jnp.int32, (points, BLK), 1).astype(F32)
    spread_ref[...] = jnp.where(lanes == column(tall, 0), 1.0, 0.0).astype(BF16)
    mass = jnp.sum(jnp.where(chosen, weights, 0.0), axis=1, keepdims=True)[:WINDOW]
    atom = start + lax.broadcasted_iota(jnp.int32, (WINDOW, 1), 0).astype(F32)
    atom = jnp.where(atom >= NATOM, atom - NATOM, atom)
    high = jnp.floor(atom * (1.0 / 16.0))
    low = atom - 16.0 * high
    lane = lax.broadcasted_iota(jnp.int32, (WINDOW, points), 1)
    facts = jnp.where(lane == 0, mass, jnp.where(lane == 1, high, jnp.where(lane == 2, low, 0.0)))
    meta_ref[...] = jnp.concatenate([jnp.zeros_like(facts), facts], axis=0)
    row = lax.broadcasted_iota(jnp.int32, (ROWS, BLK), 0)
    window = jnp.where(row == 0, high[0:1], jnp.where(row == 1, low[0:1], 0.0)).astype(BF16)
    window_ref[...] = jnp.broadcast_to(window[None], window_ref.shape)


def rows_kernel(own_ref, outer_ref, windows_ref, out_ref):
    deep, width = own_ref.shape
    lane = lax.broadcasted_iota(jnp.int32, (ROWS, width), 1)
    windows = jnp.zeros((ROWS, width), F32)
    for n in range(windows_ref.shape[0]):
        windows = jnp.where(lane == n, windows_ref[n, :, 0:1].astype(F32), windows)
    windows = windows.astype(BF16)
    for k in range(out_ref.shape[0]):
        out_ref[k, :deep] = own_ref[...]
        out_ref[k, deep : 2 * deep] = outer_ref[...]
        out_ref[k, 2 * deep :] = windows


def spread_kernel(place_ref, list_ref, *refs):
    parts = refs[:SIDE]
    kept_hbm, dense_ref, flipped_ref, sems = refs[SIDE:]
    side = len(parts)
    per, _, wide = parts[0].shape
    zl, y, group, core = (place_ref[i] for i in range(4))
    dense_ref[...] = jnp.zeros_like(dense_ref)
    flipped_ref[...] = jnp.zeros_like(flipped_ref)
    count, deep = dense_ref.shape
    owned = deep // BLK // 3
    for k, part in enumerate(parts):
        origin = lax.rem(zl - k + side, side)
        for r in range(per):
            batch = (origin * side + y) * per + r
            row = pl.multiple_of((origin * per + r) * BLK, BLK)
            for j in range(wide // BLK):
                block = list_ref[batch, j] - (group - 1) * owned
                below, above = block < owned, block >= 2 * owned
                within = jnp.where(below, block, jnp.where(above, block - 2 * owned, block - owned))
                far = jnp.where(below == (core == 0), 2, 1)
                third = jnp.where(jnp.logical_or(below, above), far, 0)
                col = pl.multiple_of((third * owned + within) * BLK, BLK)
                tile = part[r, :, j * BLK : (j + 1) * BLK]
                dense_ref[pl.ds(row, BLK), pl.ds(col, BLK)] = tile
                flipped_ref[pl.ds(col, BLK), pl.ds(row, BLK)] = tile.T
    copies = [
        pltpu.make_async_copy(dense_ref, kept_hbm.at[1, :count], sems.at[1]),
        pltpu.make_async_copy(flipped_ref, kept_hbm.at[0, :, :count], sems.at[0]),
    ]
    for copy in copies:
        copy.start()
    for copy in copies:
        copy.wait()


def psi_kernel(
    kept_hbm, near_ref, partner_ref, psi_ref, dens_ref, target_ref, dense_ref, acc_ref, sems
):
    side, deep, width = partner_ref.shape
    parts = 2
    count = dense_ref.shape[0] // parts
    loads = [
        pltpu.make_async_copy(
            kept_hbm.at[1, h * count : (h + 1) * count],
            dense_ref.at[h * count : (h + 1) * count],
            sems.at[h],
        )
        for h in range(parts)
    ]
    for load in loads:
        load.start()
    lane = lax.broadcasted_iota(jnp.int32, target_ref.shape, 1)
    device = lane // WINDOW
    atoms = (lane % WINDOW).astype(F32)
    for k in range(side):
        window = near_ref[k, 2 * deep :, :BLK].astype(F32)
        window = window[0:1] * 16.0 + window[1:2]
        for n in range(2 * side):
            atoms += jnp.where(device == n * side + k, window[:, n : n + 1], 0.0)
    target_ref[...] = jnp.where(atoms >= NATOM, atoms - NATOM, atoms)
    for h in range(parts):
        loads[h].wait()
        rows = slice(h * count, (h + 1) * count)
        for k in range(side):
            chosen = jnp.concatenate(
                [near_ref[k, :deep], partner_ref[k], near_ref[k, deep : 2 * deep]], axis=0
            )
            psi = jnp.dot(dense_ref[rows, :], chosen, preferred_element_type=F32).astype(BF16)
            psi_ref[rows, k * width : (k + 1) * width] = psi
            wide = psi.astype(F32)
            square = wide * wide
            part = square[:, :BLK] + square[:, BLK:]
            if k == 0:
                acc_ref[...] = part
            else:
                acc_ref[...] += part
        for m in range(count // BLK):
            n = h * count // BLK + m
            tile = acc_ref[m * BLK : (m + 1) * BLK, :].T
            dens_ref[n // 2, n % 2 : n % 2 + 1, :] = 2.0 * jnp.sum(tile, axis=0, keepdims=True)


def silu(x):
    return x * jax.nn.sigmoid(x)


def column(tall, n):
    return jnp.concatenate([tall[:, n : n + 1], tall[:, n + 1 : n + 2]], axis=0)


def message_of(hidden, weight, weights_col, selector, meta):
    message = silu(jnp.dot(hidden.astype(BF16), weight, preferred_element_type=F32))
    weighted = (weights_col * message).astype(BF16)
    rows = jnp.dot(selector, weighted, preferred_element_type=F32)
    return message, rows + meta


def first_kernel(
    radius_ref, pw_ref, scale_ref, shift_ref, weight_ref, sel_ref, meta_ref,
    hidden_ref, message_ref, cols_ref, out_ref, scratch,
):
    scratch[...] = jnp.zeros_like(scratch)
    scratch[0:2, :] = radius_ref[...]
    scratch[2:4, :] = pw_ref[...]
    tall = scratch[...].T
    cols_ref[...] = tall
    radius, weights = column(tall, 0), column(tall, 2)
    hidden = silu(radius * scale_ref[...] + shift_ref[...])
    hidden_ref[...] = hidden
    message, payload = message_of(hidden, weight_ref[0], weights, sel_ref[...], meta_ref[...])
    message_ref[...] = message
    out_ref[...] = jnp.broadcast_to(payload.astype(BF16)[None], out_ref.shape)


def folded(rows):
    return jnp.concatenate([rows[..., :BLK], rows[..., BLK:]], axis=-2)


def unfolded(rows):
    return jnp.concatenate([rows[:WINDOW], rows[WINDOW:]], axis=1)


def route_first_kernel(x_ref, target_ref, out_ref, match_ref):
    n = x_ref.shape[0] * ROWS
    targets = target_ref[...]
    x = x_ref[...].reshape(n, x_ref.shape[2])
    meta = x[:, :BLK].astype(F32)
    meta = jnp.concatenate([meta[WINDOW:], meta[:WINDOW]], axis=0)
    atom = meta[:, 1:2] * 16.0 + meta[:, 2:3]
    row = lax.broadcasted_iota(jnp.int32, (n, targets.shape[1]), 0)
    valid = lax.rem(row, ROWS) < WINDOW
    match = jnp.where(jnp.logical_and(atom == targets, valid), 1.0, 0.0).astype(BF16)
    match_ref[...] = match
    down = (((0,), (0,)), ((), ()))
    sums = lax.dot_general(match, x, down, preferred_element_type=F32)
    mass = lax.dot_general(match, meta.astype(BF16), down, preferred_element_type=F32)
    count = out_ref.shape[0]
    mass = jnp.concatenate([mass, jnp.zeros_like(mass)], axis=1)
    both = jnp.concatenate(
        [sums.reshape(count, WINDOW, -1), mass.reshape(count, WINDOW, -1)], axis=1
    )
    out_ref[...] = both.astype(BF16)


def route_kernel(x_ref, match_ref, out_ref):
    x = x_ref[...].reshape(x_ref.shape[0] * ROWS, x_ref.shape[2])
    wide = x.astype(F32)
    rest = jnp.concatenate([wide[WINDOW:], wide[:WINDOW]], axis=0).astype(BF16)
    down = (((0,), (0,)), ((), ()))
    halves = [
        lax.dot_general(match_ref[...], half, down, preferred_element_type=F32).reshape(
            out_ref.shape[0], WINDOW, -1
        )
        for half in (x, rest)
    ]
    out_ref[...] = jnp.concatenate(halves, axis=1).astype(BF16)


def updated(rows, mass, weight, hidden, message, spread):
    mean = rows / (1.0 + mass)
    mean = jnp.concatenate([mean, jnp.zeros_like(mean)], axis=0).astype(BF16)
    update = silu(jnp.dot(mean, weight, preferred_element_type=F32)).astype(BF16)
    filler = jnp.zeros((BLK - ROWS, update.shape[1]), BF16)
    update = jnp.concatenate([update, filler], axis=0)
    picked = jnp.dot(spread, update, preferred_element_type=F32)
    return hidden + message * picked


def second_kernel(
    z_ref, atom_weight_ref, weight_ref, hidden_ref, message_ref, cols_ref, spread_ref, sel_ref,
    hidden_out, message_out, mass_ref, out_ref,
):
    total = jnp.sum(z_ref[...].astype(F32), axis=0)
    mass = jnp.broadcast_to(total[WINDOW:, 0:1], mass_ref.shape)
    mass_ref[...] = mass
    hidden = updated(
        total[:WINDOW], mass[:, 0:1], atom_weight_ref[0], hidden_ref[...], message_ref[...],
        spread_ref[...],
    )
    hidden_out[...] = hidden
    weights = column(cols_ref[...], 2)
    message, payload = message_of(hidden, weight_ref[1], weights, sel_ref[...], 0.0)
    message_out[...] = message
    payload = folded(payload[:WINDOW]).astype(BF16)
    out_ref[...] = jnp.broadcast_to(payload[None], out_ref.shape)


def last_kernel(
    z_ref, mass_ref, atom_weight_ref, hidden_ref, message_ref, cols_ref, spread_ref, head_ref,
    potential_ref, scaled_ref,
):
    total = jnp.sum(z_ref[...].astype(F32), axis=0)
    hidden = updated(
        unfolded(total), mass_ref[:, 0:1], atom_weight_ref[1], hidden_ref[...], message_ref[...],
        spread_ref[...],
    )
    score = jnp.sum(hidden * head_ref[...], axis=1, keepdims=True)
    radius, weights = column(cols_ref[...], 0), column(cols_ref[...], 2)
    potential = radius * (1.0 + jnp.tanh(score))
    scaled = weights * potential
    lane = lax.broadcasted_iota(jnp.int32, (BLK, BLK), 1)
    flat = jnp.where(lane == 0, potential[:BLK], 0.0)
    flat = jnp.where(lane == 1, potential[BLK:], flat)
    flat = jnp.where(lane == 2, scaled[:BLK], flat)
    flat = jnp.where(lane == 3, scaled[BLK:], flat)
    flat = flat.T
    potential_ref[...] = flat[0:2]
    for k in range(scaled_ref.shape[0]):
        scaled_ref[k] = flat[2:4]


def scaled_psi(psi_ref, scaled_ref, weighted, scratch):
    side = scaled_ref.shape[0]
    for k in range(side):
        scratch[2 * k : 2 * k + 2, :] = scaled_ref[k]
    tall = scratch[...].T
    for n in range(2 * side):
        rows = slice(n * BLK, (n + 1) * BLK)
        weighted[rows, :] = (tall[:, n : n + 1] * psi_ref[rows, :].astype(F32)).astype(BF16)


def outer_kernel(
    place_ref, kept_hbm, psi_ref, scaled_ref, out_ref, weighted, flipped_ref, scratch, sem
):
    side, deep, width = out_ref.shape
    copy = pltpu.make_async_copy(kept_hbm.at[0, 2 * deep :, : psi_ref.shape[0]], flipped_ref, sem)
    copy.start()
    scaled_psi(psi_ref, scaled_ref, weighted, scratch)
    copy.wait()
    for k in range(side):
        terms = jnp.dot(
            flipped_ref[...],
            weighted[:, k * width : (k + 1) * width],
            preferred_element_type=F32,
        )
        out_ref[k] = terms.astype(BF16)


def near_kernel(
    place_ref, kept_hbm, psi_ref, scaled_ref, out_ref, weighted, flipped_ref, scratch, sem
):
    count, deep, width = out_ref.shape
    side = count // 2
    copy = pltpu.make_async_copy(kept_hbm.at[0, : 2 * deep, : psi_ref.shape[0]], flipped_ref, sem)
    copy.start()
    core = place_ref[3]
    scaled_psi(psi_ref, scaled_ref, weighted, scratch)
    copy.wait()
    for k in range(side):
        terms = jnp.dot(
            flipped_ref[...],
            weighted[:, k * width : (k + 1) * width],
            preferred_element_type=F32,
        ).astype(BF16)
        out_ref[core * side + k] = terms[:deep]
        out_ref[(1 - core) * side + k] = terms[deep:]


def from_behind(value, axis):
    return [value] + [
        lax.ppermute(value, axis, [(i, (i + k) % SIDE) for i in range(SIDE)])
        for k in range(1, SIDE)
    ]


def across(value):
    groups = lax.axis_size(GRID)
    pairs = [(g, g + 1 if g % 2 else g - 1) for g in range(1, groups - 1)]
    return lax.ppermute(value, GRID, pairs)


def swap(value):
    return lax.ppermute(value, "c", [(0, 1), (1, 0)])


def exchange(parts, axes):
    return lax.all_to_all(parts, axes, split_axis=0, concat_axis=0, tiled=True)


def local(
    basis_values,
    block_lists,
    orbitals,
    point_weights,
    point_atoms,
    embed_scale,
    embed_shift,
    message_weight,
    atom_weight,
    head_weight,
):
    feat = embed_scale.shape[0]
    points = point_weights.shape[0]
    batches, batch_points, _ = basis_values.shape
    deep, width = orbitals.shape
    place = jnp.stack([lax.axis_index(a) for a in ("zl", "y", GRID, "c")]).astype(jnp.int32)
    plane, column_size = lax.axis_size(PLANE), lax.axis_size(COLUMN)
    square_f32 = shape((points, feat), F32)

    outer = across(orbitals)
    selector, spread, meta, window = call(
        prepare_kernel,
        (
            shape((ROWS, points), BF16),
            shape((points, BLK), BF16),
            shape((ROWS, feat), F32),
            shape((2 * SIDE, ROWS, BLK), BF16),
        ),
        2,
        scratch=[pltpu.VMEM((8, batch_points), F32)],
    )(point_atoms.reshape(batches, batch_points), point_weights.reshape(batches, batch_points))
    windows = exchange(window, ("x", "c"))
    rows = call(rows_kernel, shape((SIDE, 2 * deep + ROWS, width), BF16), 3)(
        orbitals, outer, windows
    )
    total_points = SIDE * points
    everywhere = pl.BlockSpec(memory_space=pltpu.VMEM)
    scalars = pl.BlockSpec(memory_space=pltpu.SMEM)
    anywhere = pl.BlockSpec(memory_space=pl.ANY)
    kept = pl.pallas_call(
        spread_kernel,
        out_shape=shape((SPARE, 3 * deep, 3 * deep), BF16),
        in_specs=[scalars] * 2 + [everywhere] * SIDE,
        out_specs=anywhere,
        scratch_shapes=[
            pltpu.VMEM((total_points, 3 * deep), BF16),
            pltpu.VMEM((3 * deep, total_points), BF16),
            pltpu.SemaphoreType.DMA((2,)),
        ],
        compiler_params=pltpu.CompilerParams(vmem_limit_bytes=VMEM),
    )(place, block_lists, *from_behind(basis_values, "zl"))
    near, kept = lax.optimization_barrier((exchange(rows, ("y",)), kept))
    partner = swap(near[:, :deep])
    psi, squares, targets = pl.pallas_call(
        psi_kernel,
        out_shape=(
            shape((total_points, SIDE * width), BF16),
            shape((SIDE, batches, batch_points), F32),
            shape((1, plane * WINDOW), F32),
        ),
        in_specs=[anywhere, everywhere, everywhere],
        out_specs=(everywhere, everywhere, everywhere),
        scratch_shapes=[
            pltpu.VMEM((total_points, 3 * deep), BF16),
            pltpu.VMEM((total_points // 2, BLK), F32),
            pltpu.SemaphoreType.DMA((2,)),
        ],
        compiler_params=pltpu.CompilerParams(vmem_limit_bytes=VMEM),
    )(kept, near, partner)
    squares = exchange(squares, ("zl",))
    radius = jnp.cbrt(jnp.sum(squares, axis=0))

    weights = point_weights.reshape(batches, batch_points)
    to_plane = shape((plane, ROWS, feat), BF16)
    to_column = shape((column_size, ROWS, feat), BF16)
    tall = shape((batch_points, 8), F32)
    hidden, message, cols, sent = call(
        first_kernel,
        (square_f32, square_f32, tall, to_column),
        7,
        scratch=[pltpu.VMEM((8, batch_points), F32)],
    )(radius, weights, embed_scale[None], embed_shift[None], message_weight, selector, meta)
    sums, match = call(
        route_first_kernel,
        (to_plane, shape((column_size * ROWS, plane * WINDOW), BF16)),
        2,
    )(exchange(sent, COLUMN), targets)
    hidden, message, mass_rows, sent = call(
        second_kernel,
        (
            square_f32,
            square_f32,
            shape((WINDOW, BLK), F32),
            shape((column_size, ROWS, BLK), BF16),
        ),
        8,
    )(
        exchange(sums, PLANE), atom_weight, message_weight, hidden, message, cols, spread, selector
    )
    sums = call(route_kernel, shape((plane, ROWS, BLK), BF16), 2)(exchange(sent, COLUMN), match)
    potential, scaled = call(
        last_kernel,
        (shape((batches, batch_points), F32), shape((SIDE, batches, batch_points), F32)),
        8,
    )(
        exchange(sums, PLANE), mass_rows, atom_weight, hidden, message, cols, spread,
        head_weight[None],
    )
    scaled = exchange(scaled, ("zl",))

    def fock_terms(kernel, devices, rows):
        return pl.pallas_call(
            kernel,
            out_shape=shape((devices, deep, width), BF16),
            in_specs=[scalars, anywhere, everywhere, everywhere],
            out_specs=everywhere,
            scratch_shapes=[
                pltpu.VMEM((total_points, SIDE * width), BF16),
                pltpu.VMEM((rows, total_points), BF16),
                pltpu.VMEM((8, batch_points), F32),
                pltpu.SemaphoreType.DMA,
            ],
            compiler_params=pltpu.CompilerParams(vmem_limit_bytes=VMEM),
        )(place, kept, psi, scaled)

    outer = fock_terms(outer_kernel, SIDE, deep)
    near = fock_terms(near_kernel, 2 * SIDE, 2 * deep)
    arrived = across(jnp.sum(exchange(outer, ("y",)).astype(F32), axis=0).astype(BF16))
    fock = jnp.sum(exchange(near, ("c", "y")).astype(F32), axis=0) + arrived.astype(F32)
    return fock, potential.reshape(-1)


def solution(mesh):
    finer = Mesh(mesh.devices.reshape(4, 4, 2, 4, 4), AXES)
    atom = ("zl", "y")
    placed = (
        P(AXES, None, None),
        P(GRID, None),
        P(GRID, atom),
        P(AXES),
        P(AXES),
        P(),
        P(),
        P(),
        P(),
        P(),
    )
    return jax.shard_map(
        local,
        mesh=finer,
        in_specs=placed,
        out_specs=(P(GRID, atom), P(AXES)),
        check_vma=False,
    )
```

```python
import jax
import jax.numpy as jnp
from jax import lax
from jax.experimental import pallas as pl
from jax.experimental.pallas import tpu as pltpu
from jax.sharding import Mesh
from jax.sharding import PartitionSpec as P

AXES = ("x", "zh", "c", "zl", "y")
GRID = ("x", "zh", "c")
PLANE = ("x", "c", "y")
COLUMN = ("zh", "zl")
SIDE = 4
BLK = 128
WINDOW = 8
NATOM = 512
ROWS = 16
SPARE = 24
F32 = jnp.float32
BF16 = jnp.bfloat16

VMEM = 16 * 1024 * 1024


def call(kernel, out_shape, n_in, smem=(), scratch=(), **kw):
    specs = [
        pl.BlockSpec(memory_space=pltpu.SMEM if i in smem else pltpu.VMEM) for i in range(n_in)
    ]
    outs = jax.tree.map(lambda _: pl.BlockSpec(memory_space=pltpu.VMEM), out_shape)
    return pl.pallas_call(
        kernel,
        out_shape=out_shape,
        in_specs=specs,
        out_specs=outs,
        scratch_shapes=list(scratch),
        compiler_params=pltpu.CompilerParams(vmem_limit_bytes=VMEM),
        **kw,
    )


def shape(dims, dtype):
    return jax.ShapeDtypeStruct(dims, dtype)


def prepare_kernel(atoms_ref, weights_ref, sel_ref, spread_ref, meta_ref, window_ref, scratch):
    atoms = atoms_ref[...].astype(F32)
    half = NATOM // 2
    first = atoms[0:1, 0:1]
    apart = atoms - first
    apart = jnp.where(apart < -half, apart + NATOM, jnp.where(apart >= half, apart - NATOM, apart))
    start = first + jnp.min(jnp.min(apart, axis=1, keepdims=True), axis=0, keepdims=True)
    start = jnp.where(start < 0, start + NATOM, jnp.where(start >= NATOM, start - NATOM, start))
    slot = atoms - start
    slot = jnp.where(slot < 0, slot + NATOM, slot)
    points = 2 * BLK
    wide = jnp.concatenate([slot[0:1], slot[1:2]], axis=1)
    weights = jnp.concatenate([weights_ref[0:1], weights_ref[1:2]], axis=1)
    rows = lax.broadcasted_iota(jnp.int32, (ROWS, points), 0).astype(F32)
    chosen = rows == wide
    sel_ref[...] = jnp.where(chosen, 1.0, 0.0).astype(BF16)
    scratch[...] = jnp.zeros_like(scratch)
    scratch[0:2, :] = slot
    tall = scratch[...].T
    lanes = lax.broadcasted_iota(jnp.int32, (points, BLK), 1).astype(F32)
    spread_ref[...] = jnp.where(lanes == column(tall, 0), 1.0, 0.0).astype(BF16)
    mass = jnp.sum(jnp.where(chosen, weights, 0.0), axis=1, keepdims=True)[:WINDOW]
    atom = start + lax.broadcasted_iota(jnp.int32, (WINDOW, 1), 0).astype(F32)
    atom = jnp.where(atom >= NATOM, atom - NATOM, atom)
    high = jnp.floor(atom * (1.0 / 16.0))
    low = atom - 16.0 * high
    lane = lax.broadcasted_iota(jnp.int32, (WINDOW, points), 1)
    facts = jnp.where(lane == 0, mass, jnp.where(lane == 1, high, jnp.where(lane == 2, low, 0.0)))
    meta_ref[...] = jnp.concatenate([jnp.zeros_like(facts), facts], axis=0)
    row = lax.broadcasted_iota(jnp.int32, (ROWS, BLK), 0)
    window = jnp.where(row == 0, high[0:1], jnp.where(row == 1, low[0:1], 0.0)).astype(BF16)
    window_ref[...] = jnp.broadcast_to(window[None], window_ref.shape)


def rows_kernel(own_ref, outer_ref, windows_ref, out_ref):
    deep, width = own_ref.shape
    lane = lax.broadcasted_iota(jnp.int32, (ROWS, width), 1)
    windows = jnp.zeros((ROWS, width), F32)
    for n in range(windows_ref.shape[0]):
        windows = jnp.where(lane == n, windows_ref[n, :, 0:1].astype(F32), windows)
    windows = windows.astype(BF16)
    for k in range(out_ref.shape[0]):
        out_ref[k, :deep] = own_ref[...]
        out_ref[k, deep : 2 * deep] = outer_ref[...]
        out_ref[k, 2 * deep :] = windows


def spread_kernel(place_ref, list_ref, *refs):
    parts = refs[:SIDE]
    kept_hbm, dense_ref, flipped_ref, sems = refs[SIDE:]
    side = len(parts)
    per, _, wide = parts[0].shape
    zl, y, group, core = (place_ref[i] for i in range(4))
    dense_ref[...] = jnp.zeros_like(dense_ref)
    flipped_ref[...] = jnp.zeros_like(flipped_ref)
    count, deep = dense_ref.shape
    owned = deep // BLK // 3
    for k, part in enumerate(parts):
        origin = lax.rem(zl - k + side, side)
        for r in range(per):
            batch = (origin * side + y) * per + r
            row = pl.multiple_of((origin * per + r) * BLK, BLK)
            for j in range(wide // BLK):
                block = list_ref[batch, j] - (group - 1) * owned
                below, above = block < owned, block >= 2 * owned
                within = jnp.where(below, block, jnp.where(above, block - 2 * owned, block - owned))
                far = jnp.where(below == (core == 0), 2, 1)
                third = jnp.where(jnp.logical_or(below, above), far, 0)
                col = pl.multiple_of((third * owned + within) * BLK, BLK)
                tile = part[r, :, j * BLK : (j + 1) * BLK]
                dense_ref[pl.ds(row, BLK), pl.ds(col, BLK)] = tile
                flipped_ref[pl.ds(col, BLK), pl.ds(row, BLK)] = tile.T
    copies = [
        pltpu.make_async_copy(dense_ref, kept_hbm.at[1, :count], sems.at[1]),
        pltpu.make_async_copy(flipped_ref, kept_hbm.at[0, :, :count], sems.at[0]),
    ]
    for copy in copies:
        copy.start()
    for copy in copies:
        copy.wait()


def psi_kernel(
    kept_hbm, near_ref, partner_ref, psi_ref, dens_ref, target_ref, dense_ref, acc_ref, sems
):
    side, deep, width = partner_ref.shape
    parts = 2
    count = dense_ref.shape[0] // parts
    loads = [
        pltpu.make_async_copy(
            kept_hbm.at[1, h * count : (h + 1) * count],
            dense_ref.at[h * count : (h + 1) * count],
            sems.at[h],
        )
        for h in range(parts)
    ]
    for load in loads:
        load.start()
    lane = lax.broadcasted_iota(jnp.int32, target_ref.shape, 1)
    device = lane // WINDOW
    atoms = (lane % WINDOW).astype(F32)
    for k in range(side):
        window = near_ref[k, 2 * deep :, :BLK].astype(F32)
        window = window[0:1] * 16.0 + window[1:2]
        for n in range(2 * side):
            atoms += jnp.where(device == n * side + k, window[:, n : n + 1], 0.0)
    target_ref[...] = jnp.where(atoms >= NATOM, atoms - NATOM, atoms)
    for h in range(parts):
        loads[h].wait()
        rows = slice(h * count, (h + 1) * count)
        for k in range(side):
            chosen = jnp.concatenate(
                [near_ref[k, :deep], partner_ref[k], near_ref[k, deep : 2 * deep]], axis=0
            )
            psi = jnp.dot(dense_ref[rows, :], chosen, preferred_element_type=F32).astype(BF16)
            psi_ref[rows, k * width : (k + 1) * width] = psi
            wide = psi.astype(F32)
            square = wide * wide
            part = square[:, :BLK] + square[:, BLK:]
            if k == 0:
                acc_ref[...] = part
            else:
                acc_ref[...] += part
        for m in range(count // BLK):
            n = h * count // BLK + m
            tile = acc_ref[m * BLK : (m + 1) * BLK, :].T
            dens_ref[n // 2, n % 2 : n % 2 + 1, :] = 2.0 * jnp.sum(tile, axis=0, keepdims=True)


def silu(x):
    return x * jax.nn.sigmoid(x)


def column(tall, n):
    return jnp.concatenate([tall[:, n : n + 1], tall[:, n + 1 : n + 2]], axis=0)


def message_of(hidden, weight, weights_col, selector, meta):
    message = silu(jnp.dot(hidden.astype(BF16), weight, preferred_element_type=F32))
    weighted = (weights_col * message).astype(BF16)
    rows = jnp.dot(selector, weighted, preferred_element_type=F32)
    return message, rows + meta


def first_kernel(
    radius_ref, pw_ref, scale_ref, shift_ref, weight_ref, sel_ref, meta_ref,
    hidden_ref, message_ref, cols_ref, out_ref, scratch,
):
    scratch[...] = jnp.zeros_like(scratch)
    scratch[0:2, :] = radius_ref[...]
    scratch[2:4, :] = pw_ref[...]
    tall = scratch[...].T
    cols_ref[...] = tall
    radius, weights = column(tall, 0), column(tall, 2)
    hidden = silu(radius * scale_ref[...] + shift_ref[...])
    hidden_ref[...] = hidden
    message, payload = message_of(hidden, weight_ref[0], weights, sel_ref[...], meta_ref[...])
    message_ref[...] = message
    out_ref[...] = jnp.broadcast_to(payload.astype(BF16)[None], out_ref.shape)


def folded(rows):
    return jnp.concatenate([rows[..., :BLK], rows[..., BLK:]], axis=-2)


def unfolded(rows):
    return jnp.concatenate([rows[:WINDOW], rows[WINDOW:]], axis=1)


def route_first_kernel(x_ref, target_ref, out_ref, match_ref):
    n = x_ref.shape[0] * ROWS
    targets = target_ref[...]
    x = x_ref[...].reshape(n, x_ref.shape[2])
    meta = x[:, :BLK].astype(F32)
    meta = jnp.concatenate([meta[WINDOW:], meta[:WINDOW]], axis=0)
    atom = meta[:, 1:2] * 16.0 + meta[:, 2:3]
    row = lax.broadcasted_iota(jnp.int32, (n, targets.shape[1]), 0)
    valid = lax.rem(row, ROWS) < WINDOW
    match = jnp.where(jnp.logical_and(atom == targets, valid), 1.0, 0.0).astype(BF16)
    match_ref[...] = match
    down = (((0,), (0,)), ((), ()))
    sums = lax.dot_general(match, x, down, preferred_element_type=F32)
    mass = lax.dot_general(match, meta.astype(BF16), down, preferred_element_type=F32)
    count = out_ref.shape[0]
    mass = jnp.concatenate([mass, jnp.zeros_like(mass)], axis=1)
    both = jnp.concatenate(
        [sums.reshape(count, WINDOW, -1), mass.reshape(count, WINDOW, -1)], axis=1
    )
    out_ref[...] = both.astype(BF16)


def route_kernel(x_ref, match_ref, out_ref):
    x = x_ref[...].reshape(x_ref.shape[0] * ROWS, x_ref.shape[2])
    wide = x.astype(F32)
    rest = jnp.concatenate([wide[WINDOW:], wide[:WINDOW]], axis=0).astype(BF16)
    down = (((0,), (0,)), ((), ()))
    halves = [
        lax.dot_general(match_ref[...], half, down, preferred_element_type=F32).reshape(
            out_ref.shape[0], WINDOW, -1
        )
        for half in (x, rest)
    ]
    out_ref[...] = jnp.concatenate(halves, axis=1).astype(BF16)


def updated(rows, mass, weight, hidden, message, spread):
    mean = rows / (1.0 + mass)
    mean = jnp.concatenate([mean, jnp.zeros_like(mean)], axis=0).astype(BF16)
    update = silu(jnp.dot(mean, weight, preferred_element_type=F32)).astype(BF16)
    filler = jnp.zeros((BLK - ROWS, update.shape[1]), BF16)
    update = jnp.concatenate([update, filler], axis=0)
    picked = jnp.dot(spread, update, preferred_element_type=F32)
    return hidden + message * picked


def second_kernel(
    z_ref, atom_weight_ref, weight_ref, hidden_ref, message_ref, cols_ref, spread_ref, sel_ref,
    hidden_out, message_out, mass_ref, out_ref,
):
    total = jnp.sum(z_ref[...].astype(F32), axis=0)
    mass = jnp.broadcast_to(total[WINDOW:, 0:1], mass_ref.shape)
    mass_ref[...] = mass
    hidden = updated(
        total[:WINDOW], mass[:, 0:1], atom_weight_ref[0], hidden_ref[...], message_ref[...],
        spread_ref[...],
    )
    hidden_out[...] = hidden
    weights = column(cols_ref[...], 2)
    message, payload = message_of(hidden, weight_ref[1], weights, sel_ref[...], 0.0)
    message_out[...] = message
    payload = folded(payload[:WINDOW]).astype(BF16)
    out_ref[...] = jnp.broadcast_to(payload[None], out_ref.shape)


def last_kernel(
    z_ref, mass_ref, atom_weight_ref, hidden_ref, message_ref, cols_ref, spread_ref, head_ref,
    potential_ref, scaled_ref,
):
    total = jnp.sum(z_ref[...].astype(F32), axis=0)
    hidden = updated(
        unfolded(total), mass_ref[:, 0:1], atom_weight_ref[1], hidden_ref[...], message_ref[...],
        spread_ref[...],
    )
    score = jnp.sum(hidden * head_ref[...], axis=1, keepdims=True)
    radius, weights = column(cols_ref[...], 0), column(cols_ref[...], 2)
    potential = radius * (1.0 + jnp.tanh(score))
    scaled = weights * potential
    lane = lax.broadcasted_iota(jnp.int32, (BLK, BLK), 1)
    flat = jnp.where(lane == 0, potential[:BLK], 0.0)
    flat = jnp.where(lane == 1, potential[BLK:], flat)
    flat = jnp.where(lane == 2, scaled[:BLK], flat)
    flat = jnp.where(lane == 3, scaled[BLK:], flat)
    flat = flat.T
    potential_ref[...] = flat[0:2]
    for k in range(scaled_ref.shape[0]):
        scaled_ref[k] = flat[2:4]


def scaled_psi(psi_ref, scaled_ref, weighted, scratch):
    side = scaled_ref.shape[0]
    for k in range(side):
        scratch[2 * k : 2 * k + 2, :] = scaled_ref[k]
    tall = scratch[...].T
    for n in range(2 * side):
        rows = slice(n * BLK, (n + 1) * BLK)
        weighted[rows, :] = (tall[:, n : n + 1] * psi_ref[rows, :].astype(F32)).astype(BF16)


def outer_kernel(
    place_ref, kept_hbm, psi_ref, scaled_ref, out_ref, weighted, flipped_ref, scratch, sem
):
    side, deep, width = out_ref.shape
    copy = pltpu.make_async_copy(
        kept_hbm.at[0, 2 * deep :, : psi_ref.shape[0]], flipped_ref, sem
    )
    copy.start()
    scale = jnp.concatenate(
        [scaled_ref[n // 2, n % 2 : n % 2 + 1, :] for n in range(2 * side)], axis=1
    )
    copy.wait()
    flipped = (flipped_ref[...].astype(F32) * scale).astype(BF16)
    for k in range(side):
        terms = jnp.dot(
            flipped, psi_ref[:, k * width : (k + 1) * width], preferred_element_type=F32
        )
        out_ref[k] = terms.astype(BF16)


def near_kernel(
    place_ref, kept_hbm, psi_ref, scaled_ref, out_ref, weighted, flipped_ref, scratch, sem
):
    count, deep, width = out_ref.shape
    side = count // 2
    copy = pltpu.make_async_copy(kept_hbm.at[0, : 2 * deep, : psi_ref.shape[0]], flipped_ref, sem)
    copy.start()
    core = place_ref[3]
    scaled_psi(psi_ref, scaled_ref, weighted, scratch)
    copy.wait()
    for k in range(side):
        terms = jnp.dot(
            flipped_ref[...],
            weighted[:, k * width : (k + 1) * width],
            preferred_element_type=F32,
        ).astype(BF16)
        out_ref[core * side + k] = terms[:deep]
        out_ref[(1 - core) * side + k] = terms[deep:]


def from_behind(value, axis):
    return [value] + [
        lax.ppermute(value, axis, [(i, (i + k) % SIDE) for i in range(SIDE)])
        for k in range(1, SIDE)
    ]


def across(value):
    groups = lax.axis_size(GRID)
    pairs = [(g, g + 1 if g % 2 else g - 1) for g in range(1, groups - 1)]
    return lax.ppermute(value, GRID, pairs)


def swap(value):
    return lax.ppermute(value, "c", [(0, 1), (1, 0)])


def exchange(parts, axes):
    return lax.all_to_all(parts, axes, split_axis=0, concat_axis=0, tiled=True)


def local(
    basis_values,
    block_lists,
    orbitals,
    point_weights,
    point_atoms,
    embed_scale,
    embed_shift,
    message_weight,
    atom_weight,
    head_weight,
):
    feat = embed_scale.shape[0]
    points = point_weights.shape[0]
    batches, batch_points, _ = basis_values.shape
    deep, width = orbitals.shape
    place = jnp.stack([lax.axis_index(a) for a in ("zl", "y", GRID, "c")]).astype(jnp.int32)
    plane, column_size = lax.axis_size(PLANE), lax.axis_size(COLUMN)
    square_f32 = shape((points, feat), F32)

    outer = across(orbitals)
    selector, spread, meta, window = call(
        prepare_kernel,
        (
            shape((ROWS, points), BF16),
            shape((points, BLK), BF16),
            shape((ROWS, feat), F32),
            shape((2 * SIDE, ROWS, BLK), BF16),
        ),
        2,
        scratch=[pltpu.VMEM((8, batch_points), F32)],
    )(point_atoms.reshape(batches, batch_points), point_weights.reshape(batches, batch_points))
    windows = exchange(window, ("x", "c"))
    rows = call(rows_kernel, shape((SIDE, 2 * deep + ROWS, width), BF16), 3)(
        orbitals, outer, windows
    )
    total_points = SIDE * points
    everywhere = pl.BlockSpec(memory_space=pltpu.VMEM)
    scalars = pl.BlockSpec(memory_space=pltpu.SMEM)
    anywhere = pl.BlockSpec(memory_space=pl.ANY)
    kept = pl.pallas_call(
        spread_kernel,
        out_shape=shape((SPARE, 3 * deep, 3 * deep), BF16),
        in_specs=[scalars] * 2 + [everywhere] * SIDE,
        out_specs=anywhere,
        scratch_shapes=[
            pltpu.VMEM((total_points, 3 * deep), BF16),
            pltpu.VMEM((3 * deep, total_points), BF16),
            pltpu.SemaphoreType.DMA((2,)),
        ],
        compiler_params=pltpu.CompilerParams(vmem_limit_bytes=VMEM),
    )(place, block_lists, *from_behind(basis_values, "zl"))
    near, kept = lax.optimization_barrier((exchange(rows, ("y",)), kept))
    partner = swap(near[:, :deep])
    psi, squares, targets = pl.pallas_call(
        psi_kernel,
        out_shape=(
            shape((total_points, SIDE * width), BF16),
            shape((SIDE, batches, batch_points), F32),
            shape((1, plane * WINDOW), F32),
        ),
        in_specs=[anywhere, everywhere, everywhere],
        out_specs=(everywhere, everywhere, everywhere),
        scratch_shapes=[
            pltpu.VMEM((total_points, 3 * deep), BF16),
            pltpu.VMEM((total_points // 2, BLK), F32),
            pltpu.SemaphoreType.DMA((2,)),
        ],
        compiler_params=pltpu.CompilerParams(vmem_limit_bytes=VMEM),
    )(kept, near, partner)
    squares = exchange(squares, ("zl",))
    radius = jnp.cbrt(jnp.sum(squares, axis=0))

    weights = point_weights.reshape(batches, batch_points)
    to_plane = shape((plane, ROWS, feat), BF16)
    to_column = shape((column_size, ROWS, feat), BF16)
    tall = shape((batch_points, 8), F32)
    hidden, message, cols, sent = call(
        first_kernel,
        (square_f32, square_f32, tall, to_column),
        7,
        scratch=[pltpu.VMEM((8, batch_points), F32)],
    )(radius, weights, embed_scale[None], embed_shift[None], message_weight, selector, meta)
    sums, match = call(
        route_first_kernel,
        (to_plane, shape((column_size * ROWS, plane * WINDOW), BF16)),
        2,
    )(exchange(sent, COLUMN), targets)
    hidden, message, mass_rows, sent = call(
        second_kernel,
        (
            square_f32,
            square_f32,
            shape((WINDOW, BLK), F32),
            shape((column_size, ROWS, BLK), BF16),
        ),
        8,
    )(
        exchange(sums, PLANE), atom_weight, message_weight, hidden, message, cols, spread, selector
    )
    sums = call(route_kernel, shape((plane, ROWS, BLK), BF16), 2)(exchange(sent, COLUMN), match)
    potential, scaled = call(
        last_kernel,
        (shape((batches, batch_points), F32), shape((SIDE, batches, batch_points), F32)),
        8,
    )(
        exchange(sums, PLANE), mass_rows, atom_weight, hidden, message, cols, spread,
        head_weight[None],
    )
    scaled = exchange(scaled, ("zl",))

    def fock_terms(kernel, devices, rows):
        return pl.pallas_call(
            kernel,
            out_shape=shape((devices, deep, width), BF16),
            in_specs=[scalars, anywhere, everywhere, everywhere],
            out_specs=everywhere,
            scratch_shapes=[
                pltpu.VMEM((total_points, SIDE * width), BF16),
                pltpu.VMEM((rows, total_points), BF16),
                pltpu.VMEM((8, batch_points), F32),
                pltpu.SemaphoreType.DMA,
            ],
            compiler_params=pltpu.CompilerParams(vmem_limit_bytes=VMEM),
        )(place, kept, psi, scaled)

    outer = fock_terms(outer_kernel, SIDE, deep)
    near = fock_terms(near_kernel, 2 * SIDE, 2 * deep)
    arrived = across(jnp.sum(exchange(outer, ("y",)).astype(F32), axis=0).astype(BF16))
    fock = jnp.sum(exchange(near, ("c", "y")).astype(F32), axis=0) + arrived.astype(F32)
    return fock, potential.reshape(-1)


def solution(mesh):
    finer = Mesh(mesh.devices.reshape(4, 4, 2, 4, 4), AXES)
    atom = ("zl", "y")
    placed = (
        P(AXES, None, None),
        P(GRID, None),
        P(GRID, atom),
        P(AXES),
        P(AXES),
        P(),
        P(),
        P(),
        P(),
        P(),
    )
    return jax.shard_map(
        local,
        mesh=finer,
        in_specs=placed,
        out_specs=(P(GRID, atom), P(AXES)),
        check_vma=False,
    )
```

```python
import jax
import jax.numpy as jnp
from jax import lax
from jax.experimental import pallas as pl
from jax.experimental.pallas import tpu as pltpu
from jax.sharding import Mesh
from jax.sharding import PartitionSpec as P

AXES = ("x", "zh", "c", "zl", "y")
GRID = ("x", "zh", "c")
PLANE = ("x", "c", "y")
COLUMN = ("zh", "zl")
SIDE = 4
BLK = 128
WINDOW = 8
NATOM = 512
ROWS = 16
SPARE = 24
F32 = jnp.float32
BF16 = jnp.bfloat16

VMEM = 16 * 1024 * 1024


def call(kernel, out_shape, n_in, smem=(), scratch=(), **kw):
    specs = [
        pl.BlockSpec(memory_space=pltpu.SMEM if i in smem else pltpu.VMEM) for i in range(n_in)
    ]
    outs = jax.tree.map(lambda _: pl.BlockSpec(memory_space=pltpu.VMEM), out_shape)
    return pl.pallas_call(
        kernel,
        out_shape=out_shape,
        in_specs=specs,
        out_specs=outs,
        scratch_shapes=list(scratch),
        compiler_params=pltpu.CompilerParams(vmem_limit_bytes=VMEM),
        **kw,
    )


def shape(dims, dtype):
    return jax.ShapeDtypeStruct(dims, dtype)


def prepare_kernel(atoms_ref, weights_ref, sel_ref, spread_ref, meta_ref, window_ref, scratch):
    atoms = atoms_ref[...].astype(F32)
    half = NATOM // 2
    first = atoms[0:1, 0:1]
    apart = atoms - first
    apart = jnp.where(apart < -half, apart + NATOM, jnp.where(apart >= half, apart - NATOM, apart))
    start = first + jnp.min(jnp.min(apart, axis=1, keepdims=True), axis=0, keepdims=True)
    start = jnp.where(start < 0, start + NATOM, jnp.where(start >= NATOM, start - NATOM, start))
    slot = atoms - start
    slot = jnp.where(slot < 0, slot + NATOM, slot)
    points = 2 * BLK
    wide = jnp.concatenate([slot[0:1], slot[1:2]], axis=1)
    weights = jnp.concatenate([weights_ref[0:1], weights_ref[1:2]], axis=1)
    rows = lax.broadcasted_iota(jnp.int32, (ROWS, points), 0).astype(F32)
    chosen = rows == wide
    sel_ref[...] = jnp.where(chosen, 1.0, 0.0).astype(BF16)
    scratch[...] = jnp.zeros_like(scratch)
    scratch[0:2, :] = slot
    tall = scratch[...].T
    lanes = lax.broadcasted_iota(jnp.int32, (points, BLK), 1).astype(F32)
    spread_ref[...] = jnp.where(lanes == column(tall, 0), 1.0, 0.0).astype(BF16)
    mass = jnp.sum(jnp.where(chosen, weights, 0.0), axis=1, keepdims=True)[:WINDOW]
    atom = start + lax.broadcasted_iota(jnp.int32, (WINDOW, 1), 0).astype(F32)
    atom = jnp.where(atom >= NATOM, atom - NATOM, atom)
    high = jnp.floor(atom * (1.0 / 16.0))
    low = atom - 16.0 * high
    lane = lax.broadcasted_iota(jnp.int32, (WINDOW, points), 1)
    facts = jnp.where(lane == 0, mass, jnp.where(lane == 1, high, jnp.where(lane == 2, low, 0.0)))
    meta_ref[...] = jnp.concatenate([jnp.zeros_like(facts), facts], axis=0)
    row = lax.broadcasted_iota(jnp.int32, (ROWS, BLK), 0)
    window = jnp.where(row == 0, high[0:1], jnp.where(row == 1, low[0:1], 0.0)).astype(BF16)
    window_ref[...] = jnp.broadcast_to(window[None], window_ref.shape)


def rows_kernel(own_ref, outer_ref, windows_ref, out_ref):
    deep, width = own_ref.shape
    lane = lax.broadcasted_iota(jnp.int32, (ROWS, width), 1)
    windows = jnp.zeros((ROWS, width), F32)
    for n in range(windows_ref.shape[0]):
        windows = jnp.where(lane == n, windows_ref[n, :, 0:1].astype(F32), windows)
    windows = windows.astype(BF16)
    for k in range(out_ref.shape[0]):
        out_ref[k, :deep] = own_ref[...]
        out_ref[k, deep : 2 * deep] = outer_ref[...]
        out_ref[k, 2 * deep :] = windows


def spread_kernel(place_ref, list_ref, *refs):
    parts = refs[:SIDE]
    kept_hbm, dense_ref, flipped_ref, sems = refs[SIDE:]
    side = len(parts)
    per, _, wide = parts[0].shape
    zl, y, group, core = (place_ref[i] for i in range(4))
    dense_ref[...] = jnp.zeros_like(dense_ref)
    flipped_ref[...] = jnp.zeros_like(flipped_ref)
    count, deep = dense_ref.shape
    owned = deep // BLK // 3
    copies = []
    for k, part in enumerate(parts):
        origin = lax.rem(zl - k + side, side)
        for r in range(per):
            batch = (origin * side + y) * per + r
            row = pl.multiple_of((origin * per + r) * BLK, BLK)
            for j in range(wide // BLK):
                block = list_ref[batch, j] - (group - 1) * owned
                below, above = block < owned, block >= 2 * owned
                within = jnp.where(below, block, jnp.where(above, block - 2 * owned, block - owned))
                far = jnp.where(below == (core == 0), 2, 1)
                third = jnp.where(jnp.logical_or(below, above), far, 0)
                col = pl.multiple_of((third * owned + within) * BLK, BLK)
                tile = part[r, :, j * BLK : (j + 1) * BLK]
                dense_ref[pl.ds(row, BLK), pl.ds(col, BLK)] = tile
                flipped_ref[pl.ds(col, BLK), pl.ds(row, BLK)] = tile.T
        rows = pl.ds(pl.multiple_of(origin * per * BLK, per * BLK), per * BLK)
        copies.append(
            pltpu.make_async_copy(dense_ref.at[rows], kept_hbm.at[1, rows], sems.at[1 + k])
        )
        copies[k].start()
    copies.append(pltpu.make_async_copy(flipped_ref, kept_hbm.at[0, :, :count], sems.at[0]))
    copies[side].start()
    for copy in copies:
        copy.wait()


def psi_kernel(
    kept_hbm, near_ref, partner_ref, psi_ref, dens_ref, target_ref, dense_ref, acc_ref, sems
):
    side, deep, width = partner_ref.shape
    parts = 2
    count = dense_ref.shape[0] // parts
    loads = [
        pltpu.make_async_copy(
            kept_hbm.at[1, h * count : (h + 1) * count],
            dense_ref.at[h * count : (h + 1) * count],
            sems.at[h],
        )
        for h in range(parts)
    ]
    for load in loads:
        load.start()
    lane = lax.broadcasted_iota(jnp.int32, target_ref.shape, 1)
    device = lane // WINDOW
    atoms = (lane % WINDOW).astype(F32)
    for k in range(side):
        window = near_ref[k, 2 * deep :, :BLK].astype(F32)
        window = window[0:1] * 16.0 + window[1:2]
        for n in range(2 * side):
            atoms += jnp.where(device == n * side + k, window[:, n : n + 1], 0.0)
    target_ref[...] = jnp.where(atoms >= NATOM, atoms - NATOM, atoms)
    for h in range(parts):
        loads[h].wait()
        rows = slice(h * count, (h + 1) * count)
        for k in range(side):
            chosen = jnp.concatenate(
                [near_ref[k, :deep], partner_ref[k], near_ref[k, deep : 2 * deep]], axis=0
            )
            psi = jnp.dot(dense_ref[rows, :], chosen, preferred_element_type=F32).astype(BF16)
            psi_ref[rows, k * width : (k + 1) * width] = psi
            wide = psi.astype(F32)
            square = wide * wide
            part = square[:, :BLK] + square[:, BLK:]
            if k == 0:
                acc_ref[...] = part
            else:
                acc_ref[...] += part
        for m in range(count // BLK):
            n = h * count // BLK + m
            tile = acc_ref[m * BLK : (m + 1) * BLK, :].T
            dens_ref[n // 2, n % 2 : n % 2 + 1, :] = 2.0 * jnp.sum(tile, axis=0, keepdims=True)


def silu(x):
    return x * jax.nn.sigmoid(x)


def column(tall, n):
    return jnp.concatenate([tall[:, n : n + 1], tall[:, n + 1 : n + 2]], axis=0)


def message_of(hidden, weight, weights_col, selector, meta):
    message = silu(jnp.dot(hidden.astype(BF16), weight, preferred_element_type=F32))
    weighted = (weights_col * message).astype(BF16)
    rows = jnp.dot(selector, weighted, preferred_element_type=F32)
    return message, rows + meta


def first_kernel(
    radius_ref, pw_ref, scale_ref, shift_ref, weight_ref, sel_ref, meta_ref,
    hidden_ref, message_ref, cols_ref, out_ref, scratch,
):
    scratch[...] = jnp.zeros_like(scratch)
    scratch[0:2, :] = radius_ref[...]
    scratch[2:4, :] = pw_ref[...]
    tall = scratch[...].T
    cols_ref[...] = tall
    radius, weights = column(tall, 0), column(tall, 2)
    hidden = silu(radius * scale_ref[...] + shift_ref[...])
    hidden_ref[...] = hidden
    message, payload = message_of(hidden, weight_ref[0], weights, sel_ref[...], meta_ref[...])
    message_ref[...] = message
    out_ref[...] = jnp.broadcast_to(payload.astype(BF16)[None], out_ref.shape)


def folded(rows):
    return jnp.concatenate([rows[..., :BLK], rows[..., BLK:]], axis=-2)


def unfolded(rows):
    return jnp.concatenate([rows[:WINDOW], rows[WINDOW:]], axis=1)


def route_first_kernel(x_ref, target_ref, out_ref, match_ref):
    n = x_ref.shape[0] * ROWS
    targets = target_ref[...]
    x = x_ref[...].reshape(n, x_ref.shape[2])
    meta = x[:, :BLK].astype(F32)
    meta = jnp.concatenate([meta[WINDOW:], meta[:WINDOW]], axis=0)
    atom = meta[:, 1:2] * 16.0 + meta[:, 2:3]
    row = lax.broadcasted_iota(jnp.int32, (n, targets.shape[1]), 0)
    valid = lax.rem(row, ROWS) < WINDOW
    match = jnp.where(jnp.logical_and(atom == targets, valid), 1.0, 0.0).astype(BF16)
    match_ref[...] = match
    down = (((0,), (0,)), ((), ()))
    sums = lax.dot_general(match, x, down, preferred_element_type=F32)
    mass = lax.dot_general(match, meta.astype(BF16), down, preferred_element_type=F32)
    count = out_ref.shape[0]
    mass = jnp.concatenate([mass, jnp.zeros_like(mass)], axis=1)
    both = jnp.concatenate(
        [sums.reshape(count, WINDOW, -1), mass.reshape(count, WINDOW, -1)], axis=1
    )
    out_ref[...] = both.astype(BF16)


def route_kernel(x_ref, match_ref, out_ref):
    x = x_ref[...].reshape(x_ref.shape[0] * ROWS, x_ref.shape[2])
    wide = x.astype(F32)
    rest = jnp.concatenate([wide[WINDOW:], wide[:WINDOW]], axis=0).astype(BF16)
    down = (((0,), (0,)), ((), ()))
    halves = [
        lax.dot_general(match_ref[...], half, down, preferred_element_type=F32).reshape(
            out_ref.shape[0], WINDOW, -1
        )
        for half in (x, rest)
    ]
    out_ref[...] = jnp.concatenate(halves, axis=1).astype(BF16)


def updated(rows, mass, weight, hidden, message, spread):
    mean = rows / (1.0 + mass)
    mean = jnp.concatenate([mean, jnp.zeros_like(mean)], axis=0).astype(BF16)
    update = silu(jnp.dot(mean, weight, preferred_element_type=F32)).astype(BF16)
    filler = jnp.zeros((BLK - ROWS, update.shape[1]), BF16)
    update = jnp.concatenate([update, filler], axis=0)
    picked = jnp.dot(spread, update, preferred_element_type=F32)
    return hidden + message * picked


def second_kernel(
    z_ref, atom_weight_ref, weight_ref, hidden_ref, message_ref, cols_ref, spread_ref, sel_ref,
    hidden_out, message_out, mass_ref, out_ref,
):
    total = jnp.sum(z_ref[...].astype(F32), axis=0)
    mass = jnp.broadcast_to(total[WINDOW:, 0:1], mass_ref.shape)
    mass_ref[...] = mass
    hidden = updated(
        total[:WINDOW], mass[:, 0:1], atom_weight_ref[0], hidden_ref[...], message_ref[...],
        spread_ref[...],
    )
    hidden_out[...] = hidden
    weights = column(cols_ref[...], 2)
    message, payload = message_of(hidden, weight_ref[1], weights, sel_ref[...], 0.0)
    message_out[...] = message
    payload = folded(payload[:WINDOW]).astype(BF16)
    out_ref[...] = jnp.broadcast_to(payload[None], out_ref.shape)


def last_kernel(
    z_ref, mass_ref, atom_weight_ref, hidden_ref, message_ref, cols_ref, spread_ref, head_ref,
    potential_ref, scaled_ref,
):
    total = jnp.sum(z_ref[...].astype(F32), axis=0)
    hidden = updated(
        unfolded(total), mass_ref[:, 0:1], atom_weight_ref[1], hidden_ref[...], message_ref[...],
        spread_ref[...],
    )
    score = jnp.sum(hidden * head_ref[...], axis=1, keepdims=True)
    radius, weights = column(cols_ref[...], 0), column(cols_ref[...], 2)
    potential = radius * (1.0 + jnp.tanh(score))
    scaled = weights * potential
    lane = lax.broadcasted_iota(jnp.int32, (BLK, BLK), 1)
    flat = jnp.where(lane == 0, potential[:BLK], 0.0)
    flat = jnp.where(lane == 1, potential[BLK:], flat)
    flat = jnp.where(lane == 2, scaled[:BLK], flat)
    flat = jnp.where(lane == 3, scaled[BLK:], flat)
    flat = flat.T
    potential_ref[...] = flat[0:2]
    for k in range(scaled_ref.shape[0]):
        scaled_ref[k] = flat[2:4]


def scaled_psi(psi_ref, scaled_ref, weighted, scratch):
    side = scaled_ref.shape[0]
    for k in range(side):
        scratch[2 * k : 2 * k + 2, :] = scaled_ref[k]
    tall = scratch[...].T
    for n in range(2 * side):
        rows = slice(n * BLK, (n + 1) * BLK)
        weighted[rows, :] = (tall[:, n : n + 1] * psi_ref[rows, :].astype(F32)).astype(BF16)


def outer_kernel(
    place_ref, kept_hbm, psi_ref, scaled_ref, out_ref, weighted, flipped_ref, scratch, sem
):
    side, deep, width = out_ref.shape
    copy = pltpu.make_async_copy(
        kept_hbm.at[0, 2 * deep :, : psi_ref.shape[0]], flipped_ref, sem
    )
    copy.start()
    scale = jnp.concatenate(
        [scaled_ref[n // 2, n % 2 : n % 2 + 1, :] for n in range(2 * side)], axis=1
    )
    copy.wait()
    flipped = (flipped_ref[...].astype(F32) * scale).astype(BF16)
    for k in range(side):
        terms = jnp.dot(
            flipped, psi_ref[:, k * width : (k + 1) * width], preferred_element_type=F32
        )
        out_ref[k] = terms.astype(BF16)


def near_kernel(
    place_ref, kept_hbm, psi_ref, scaled_ref, out_ref, weighted, flipped_ref, scratch, sem
):
    count, deep, width = out_ref.shape
    side = count // 2
    copy = pltpu.make_async_copy(kept_hbm.at[0, : 2 * deep, : psi_ref.shape[0]], flipped_ref, sem)
    copy.start()
    core = place_ref[3]
    scaled_psi(psi_ref, scaled_ref, weighted, scratch)
    copy.wait()
    for k in range(side):
        terms = jnp.dot(
            flipped_ref[...],
            weighted[:, k * width : (k + 1) * width],
            preferred_element_type=F32,
        ).astype(BF16)
        out_ref[core * side + k] = terms[:deep]
        out_ref[(1 - core) * side + k] = terms[deep:]


def from_behind(value, axis):
    return [value] + [
        lax.ppermute(value, axis, [(i, (i + k) % SIDE) for i in range(SIDE)])
        for k in range(1, SIDE)
    ]


def across(value):
    groups = lax.axis_size(GRID)
    pairs = [(g, g + 1 if g % 2 else g - 1) for g in range(1, groups - 1)]
    return lax.ppermute(value, GRID, pairs)


def swap(value):
    return lax.ppermute(value, "c", [(0, 1), (1, 0)])


def exchange(parts, axes):
    return lax.all_to_all(parts, axes, split_axis=0, concat_axis=0, tiled=True)


def local(
    basis_values,
    block_lists,
    orbitals,
    point_weights,
    point_atoms,
    embed_scale,
    embed_shift,
    message_weight,
    atom_weight,
    head_weight,
):
    feat = embed_scale.shape[0]
    points = point_weights.shape[0]
    batches, batch_points, _ = basis_values.shape
    deep, width = orbitals.shape
    place = jnp.stack([lax.axis_index(a) for a in ("zl", "y", GRID, "c")]).astype(jnp.int32)
    plane, column_size = lax.axis_size(PLANE), lax.axis_size(COLUMN)
    square_f32 = shape((points, feat), F32)

    outer = across(orbitals)
    selector, spread, meta, window = call(
        prepare_kernel,
        (
            shape((ROWS, points), BF16),
            shape((points, BLK), BF16),
            shape((ROWS, feat), F32),
            shape((2 * SIDE, ROWS, BLK), BF16),
        ),
        2,
        scratch=[pltpu.VMEM((8, batch_points), F32)],
    )(point_atoms.reshape(batches, batch_points), point_weights.reshape(batches, batch_points))
    windows = exchange(window, ("x", "c"))
    rows = call(rows_kernel, shape((SIDE, 2 * deep + ROWS, width), BF16), 3)(
        orbitals, outer, windows
    )
    total_points = SIDE * points
    everywhere = pl.BlockSpec(memory_space=pltpu.VMEM)
    scalars = pl.BlockSpec(memory_space=pltpu.SMEM)
    anywhere = pl.BlockSpec(memory_space=pl.ANY)
    kept = pl.pallas_call(
        spread_kernel,
        out_shape=shape((SPARE, 3 * deep, 3 * deep), BF16),
        in_specs=[scalars] * 2 + [everywhere] * SIDE,
        out_specs=anywhere,
        scratch_shapes=[
            pltpu.VMEM((total_points, 3 * deep), BF16),
            pltpu.VMEM((3 * deep, total_points), BF16),
            pltpu.SemaphoreType.DMA((SIDE + 1,)),
        ],
        compiler_params=pltpu.CompilerParams(vmem_limit_bytes=VMEM),
    )(place, block_lists, *from_behind(basis_values, "zl"))
    near, kept = lax.optimization_barrier((exchange(rows, ("y",)), kept))
    partner = swap(near[:, :deep])
    psi, squares, targets = pl.pallas_call(
        psi_kernel,
        out_shape=(
            shape((total_points, SIDE * width), BF16),
            shape((SIDE, batches, batch_points), F32),
            shape((1, plane * WINDOW), F32),
        ),
        in_specs=[anywhere, everywhere, everywhere],
        out_specs=(everywhere, everywhere, everywhere),
        scratch_shapes=[
            pltpu.VMEM((total_points, 3 * deep), BF16),
            pltpu.VMEM((total_points // 2, BLK), F32),
            pltpu.SemaphoreType.DMA((2,)),
        ],
        compiler_params=pltpu.CompilerParams(vmem_limit_bytes=VMEM),
    )(kept, near, partner)
    squares = exchange(squares, ("zl",))
    radius = jnp.cbrt(jnp.sum(squares, axis=0))

    weights = point_weights.reshape(batches, batch_points)
    to_plane = shape((plane, ROWS, feat), BF16)
    to_column = shape((column_size, ROWS, feat), BF16)
    tall = shape((batch_points, 8), F32)
    hidden, message, cols, sent = call(
        first_kernel,
        (square_f32, square_f32, tall, to_column),
        7,
        scratch=[pltpu.VMEM((8, batch_points), F32)],
    )(radius, weights, embed_scale[None], embed_shift[None], message_weight, selector, meta)
    sums, match = call(
        route_first_kernel,
        (to_plane, shape((column_size * ROWS, plane * WINDOW), BF16)),
        2,
    )(exchange(sent, COLUMN), targets)
    hidden, message, mass_rows, sent = call(
        second_kernel,
        (
            square_f32,
            square_f32,
            shape((WINDOW, BLK), F32),
            shape((column_size, ROWS, BLK), BF16),
        ),
        8,
    )(
        exchange(sums, PLANE), atom_weight, message_weight, hidden, message, cols, spread, selector
    )
    sums = call(route_kernel, shape((plane, ROWS, BLK), BF16), 2)(exchange(sent, COLUMN), match)
    potential, scaled = call(
        last_kernel,
        (shape((batches, batch_points), F32), shape((SIDE, batches, batch_points), F32)),
        8,
    )(
        exchange(sums, PLANE), mass_rows, atom_weight, hidden, message, cols, spread,
        head_weight[None],
    )
    scaled = exchange(scaled, ("zl",))

    def fock_terms(kernel, devices, rows):
        return pl.pallas_call(
            kernel,
            out_shape=shape((devices, deep, width), BF16),
            in_specs=[scalars, anywhere, everywhere, everywhere],
            out_specs=everywhere,
            scratch_shapes=[
                pltpu.VMEM((total_points, SIDE * width), BF16),
                pltpu.VMEM((rows, total_points), BF16),
                pltpu.VMEM((8, batch_points), F32),
                pltpu.SemaphoreType.DMA,
            ],
            compiler_params=pltpu.CompilerParams(vmem_limit_bytes=VMEM),
        )(place, kept, psi, scaled)

    outer = fock_terms(outer_kernel, SIDE, deep)
    near = fock_terms(near_kernel, 2 * SIDE, 2 * deep)
    arrived = across(jnp.sum(exchange(outer, ("y",)).astype(F32), axis=0).astype(BF16))
    fock = jnp.sum(exchange(near, ("c", "y")).astype(F32), axis=0) + arrived.astype(F32)
    return fock, potential.reshape(-1)


def solution(mesh):
    finer = Mesh(mesh.devices.reshape(4, 4, 2, 4, 4), AXES)
    atom = ("zl", "y")
    placed = (
        P(AXES, None, None),
        P(GRID, None),
        P(GRID, atom),
        P(AXES),
        P(AXES),
        P(),
        P(),
        P(),
        P(),
        P(),
    )
    return jax.shard_map(
        local,
        mesh=finer,
        in_specs=placed,
        out_specs=(P(GRID, atom), P(AXES)),
        check_vma=False,
    )
```
